512 devices in a mesh: row: 32 (over z_lo, y, core), col: 16 (over x, z_hi).
Axes of the slice: x: 4, y: 4, z: 16 (z_hi: 4, z_lo: 4; z = z_hi * 4 + z_lo), core: 2. Of those that a mesh axis runs over, the one named last changes fastest.
Arguments:
- pair_input: bfloat16 [384, 384, 128], P('row', 'col'), may hold values from -6 to 6
- pair_mask: int32 [384, 384], P('row', 'col'), may hold values from 0 to 1, as said below
- out_norm_gain: float32 [128], replicated, may hold values from 0.1 to 1.9
- out_w_in: bfloat16 [128, 640], replicated, may hold values from -0.5 to 0.5
- out_final_gain: float32 [128], replicated, may hold values from 0.1 to 1.9
- out_w_out: bfloat16 [128, 128], replicated, may hold values from -0.5 to 0.5
- in_norm_gain: float32 [128], replicated, may hold values from 0.1 to 1.9
- in_w_in: bfloat16 [128, 640], replicated, may hold values from -0.5 to 0.5
- in_final_gain: float32 [128], replicated, may hold values from 0.1 to 1.9
- in_w_out: bfloat16 [128, 128], replicated, may hold values from -0.5 to 0.5
Outputs:
- pair_output: bfloat16 [384, 384, 128], P('row', 'col')
The draws below stay inside these ranges and needn't reach their ends.
Inputs may be any that keep to these rules, and one draw needn't show every extreme that they name: pair_mask[i, j] = m[i] m[j] for a 0/1 mask m over the 384 tokens; token 0 is real and the last token is padding.
All inputs are finite; a program needn't handle non-finite values.
Results may differ from the reference program's by a relative error of at most 0.017.
Values may be sent and summed in bfloat16 or wider, within the bound.
No kernel may reach another device: no remote copies, remote signals or barrier semaphores. Data moves between devices by JAX's collectives and lax.ppermute only.
A program may use at most 64 MiB of HBM per device.

```python
import jax
import jax.numpy as jnp
from jax import lax

C = 128
N = 384


def draw_pair_mask(key, part):
    key = jax.random.fold_in(key, 11)
    drawn = jax.random.randint(key, (N,), 0, 8)
    places = jnp.arange(N)
    tokens = ((drawn > 0) | (places == 0)) & (places < N - 1)
    return (tokens[:, None] & tokens[None, :]).astype(jnp.int32)


def block_levels(stream_key, shape, pieces, least, largest):
    level = 1.0
    for axis_at, parts in pieces:
        steps = jax.random.uniform(jax.random.fold_in(jax.random.fold_in(stream_key, 6), axis_at), (parts,), jnp.float32, least / len(pieces), largest / len(pieces))
        level = level * jnp.repeat(jnp.exp(steps), shape[axis_at] // parts).reshape((-1,) + (1,) * (len(shape) - 1 - axis_at))
    return level


def gaussian(rng, shape, scale, reach, pieces=(), dtype=jnp.bfloat16):
    level = block_levels(rng, shape, pieces, -0.22, 0.18) if pieces else 1.0
    values = jax.random.normal(rng, shape, jnp.float32) * scale * level
    return jnp.minimum(jnp.maximum(values, -reach), reach).astype(dtype)


def setup_inputs(seed: int = 0) -> dict:
    seeds = jax.random.split(jax.random.key(seed), 11)
    pair_input = gaussian(seeds[0], (N, N, C), 1.0, 6.0, ((0, 32), (1, 16)))
    pair_mask = draw_pair_mask(jax.random.fold_in(seeds[10], 71), 0)
    out_norm_gain = jnp.clip(1.0 + 0.18 * jax.random.normal(seeds[2], (C,), jnp.float32), 0.1, 1.9)
    out_w_in = gaussian(seeds[3], (C, 5 * C), C ** -0.5, 0.5)
    out_final_gain = jnp.clip(1.0 + 0.18 * jax.random.normal(seeds[4], (C,), jnp.float32), 0.1, 1.9)
    out_w_out = gaussian(seeds[5], (C, C), C ** -0.5, 0.5)
    in_norm_gain = jnp.clip(1.0 + 0.18 * jax.random.normal(seeds[6], (C,), jnp.float32), 0.1, 1.9)
    in_w_in = gaussian(seeds[7], (C, 5 * C), C ** -0.5, 0.5)
    in_final_gain = jnp.clip(1.0 + 0.18 * jax.random.normal(seeds[8], (C,), jnp.float32), 0.1, 1.9)
    in_w_out = gaussian(seeds[9], (C, C), C ** -0.5, 0.5)
    return dict(pair_input=pair_input, pair_mask=pair_mask, out_norm_gain=out_norm_gain, out_w_in=out_w_in, out_final_gain=out_final_gain, out_w_out=out_w_out, in_norm_gain=in_norm_gain, in_w_in=in_w_in, in_final_gain=in_final_gain, in_w_out=in_w_out)


def layer_norm(values, gain):
    center = values - lax.optimization_barrier(jnp.mean(values, axis=-1, keepdims=True))
    spread = lax.optimization_barrier(jnp.mean(center * center, axis=-1, keepdims=True))
    return center * jax.lax.rsqrt(spread + 1e-05) * gain

def project(pair, pair_mask, norm_gain, w_in):
    width = pair.shape[-1]
    normed = layer_norm(pair.astype(jnp.float32), norm_gain).astype(jnp.bfloat16)
    proj = jnp.dot(normed, w_in, preferred_element_type=jnp.float32)
    weight = pair_mask.astype(jnp.float32)[..., None]
    left_proj = (proj[..., :width] * jax.nn.sigmoid(proj[..., 2 * width:3 * width]) * weight).astype(jnp.bfloat16)
    right_proj = (proj[..., width:2 * width] * jax.nn.sigmoid(proj[..., 3 * width:4 * width]) * weight).astype(jnp.bfloat16)
    out_gate = jax.nn.sigmoid(proj[..., 4 * width:])
    return (left_proj, right_proj, out_gate)

def finish(pair, tri_sum, out_gate, final_gain, w_out):
    final = layer_norm(tri_sum, final_gain).astype(jnp.bfloat16)
    update = jnp.dot(final, w_out, preferred_element_type=jnp.float32) * out_gate
    return (pair.astype(jnp.float32) + update).astype(jnp.bfloat16)

def reference(pair_input, pair_mask, out_norm_gain, out_w_in, out_final_gain, out_w_out, in_norm_gain, in_w_in, in_final_gain, in_w_out):
    left_proj, right_proj, out_gate = project(pair_input, pair_mask, out_norm_gain, out_w_in)
    tri_sum = jnp.einsum('ikc,jkc->ijc', left_proj.astype(jnp.float32), right_proj.astype(jnp.float32))
    middle = finish(pair_input, tri_sum, out_gate, out_final_gain, out_w_out)
    left_proj, right_proj, out_gate = project(middle, pair_mask, in_norm_gain, in_w_in)
    tri_sum = jnp.einsum('kic,kjc->ijc', left_proj.astype(jnp.float32), right_proj.astype(jnp.float32))
    return finish(middle, tri_sum, out_gate, in_final_gain, in_w_out)
```

```python
import jax
import jax.numpy as jnp
import numpy as np
from jax import lax
from jax.experimental import pallas as pl
from jax.experimental.pallas import tpu as pltpu
from jax.sharding import Mesh
from jax.sharding import PartitionSpec as P

ROW = ("zl", "y", "core")
COL = ("x", "zh")
SIZES = {"zl": 4, "y": 4, "core": 2, "x": 4, "zh": 4}
CHANNEL = ("zl", "x", "y", "core")
LINE = ("zl", "zh")
PLANE = ("x", "y", "core")

ROWS, COLS, WIDTH = 12, 24, 128
TILE = ROWS * COLS
N = 384
F32, BF16 = jnp.float32, jnp.bfloat16


def one_hot(places):
    table = np.zeros((len(places), len(places)), np.float32)
    table[np.arange(len(places)), places] = 1
    return table


def sender_order(names):
    index = np.arange(128).reshape([SIZES[a] for a in CHANNEL])
    return index.transpose([CHANNEL.index(a) for a in names]).reshape(-1)


def layer_norm(values, gain):
    center = values - jnp.mean(values, axis=-1, keepdims=True)
    spread = jnp.mean(center * center, axis=-1, keepdims=True)
    return center * lax.rsqrt(spread + 1e-05) * gain


def flat_mask(mask):
    return jnp.concatenate([mask[i : i + 1] for i in range(ROWS)], axis=1)


def project(normed, mask, w_in):
    proj = lax.dot_general(
        w_in[:, : 4 * WIDTH], normed, (((0,), (1,)), ((), ())), preferred_element_type=F32
    )
    left = proj[:WIDTH] * jax.nn.sigmoid(proj[2 * WIDTH : 3 * WIDTH]) * mask
    right = proj[WIDTH : 2 * WIDTH] * jax.nn.sigmoid(proj[3 * WIDTH : 4 * WIDTH]) * mask
    return jnp.concatenate([left, right], axis=1).astype(BF16)


def update(pair, tri, norm_gain, w_in, final_gain, w_out):
    tri = tri.astype(F32)
    tri = jnp.concatenate([tri[:, i * TILE : (i + 1) * TILE] for i in range(4)], axis=0)
    final = layer_norm(tri.T, final_gain).astype(BF16)
    normed = layer_norm(pair, norm_gain).astype(BF16)
    gate = jax.nn.sigmoid(jnp.dot(normed, w_in[:, 4 * WIDTH :], preferred_element_type=F32))
    return (pair + jnp.dot(final, w_out, preferred_element_type=F32) * gate).astype(BF16)


def first_kernel(pair_ref, norm_gain, w_in, sent):
    pair = pair_ref[:TILE].astype(F32)
    mask = flat_mask(pair_ref[TILE : TILE + 16, :].astype(F32)[:ROWS, :COLS])
    normed = layer_norm(pair, norm_gain[...]).astype(BF16)
    sent[...] = project(normed, mask, w_in)


def middle_kernel(
    pair_ref, tri, norm_gain, w_in, final_gain, w_out, next_gain, next_w_in, middle, sent
):
    pair = pair_ref[:TILE].astype(F32)
    mask = flat_mask(pair_ref[TILE : TILE + 16, :].astype(F32)[:ROWS, :COLS])
    new = update(pair, tri[...], norm_gain[...], w_in, final_gain[...], w_out[...])
    middle[...] = new
    normed = layer_norm(new.astype(F32), next_gain[...]).astype(BF16)
    sent[...] = project(normed, mask, next_w_in)


def last_kernel(pair_ref, tri, norm_gain, w_in, final_gain, w_out, out):
    pair = pair_ref[...].astype(F32)
    out[...] = update(pair, tri[...], norm_gain[...], w_in, final_gain[...], w_out[...])


def pack(sums, swapped, out):
    for zh in range(4):
        strips = []
        for x in range(4):
            at = (x * 4 + zh) * COLS
            strips.append(
                jnp.concatenate(
                    [sums[i * 32 : (i + 1) * 32, at : at + COLS] for i in range(ROWS)], axis=1
                )
            )
        for zl in range(4):
            piece = jnp.concatenate([s[zl * 8 : (zl + 1) * 8] for s in strips], axis=0)
            rest = jnp.concatenate([piece[g * 8 : (g + 1) * 8, 256:] for g in range(4)], axis=1)
            place = zh * 4 + zl if swapped else zl * 4 + zh
            out[place] = jnp.concatenate([piece[:, :128], piece[:, 128:256], rest], axis=0).astype(BF16)


def outgoing_kernel(got, senders, rows, out):
    got = jnp.dot(senders[...], got[...], preferred_element_type=F32)

    def operand(at):
        return jnp.concatenate(
            [
                jnp.concatenate(
                    [got[x * 32 : (x + 1) * 32, at + i * COLS : at + (i + 1) * COLS] for x in range(4)],
                    axis=1,
                )
                for i in range(ROWS)
            ],
            axis=0,
        ).astype(BF16)

    left, right = operand(0), operand(TILE)
    right = jnp.dot(rows[...], right, preferred_element_type=F32).astype(BF16)
    sums = lax.dot_general(left, right, (((1,), (1,)), ((), ())), preferred_element_type=F32)
    pack(sums, True, out)


def incoming_kernel(got, senders, rows, out):
    got = jnp.dot(senders[...], got[...], preferred_element_type=F32)

    def operand(at):
        return jnp.concatenate(
            [
                jnp.concatenate(
                    [got[g * 8 : (g + 1) * 8, at + k * COLS : at + (k + 1) * COLS] for g in range(16)],
                    axis=1,
                )
                for k in range(ROWS)
            ],
            axis=0,
        ).astype(BF16)

    left, right = operand(0), operand(TILE)
    left = lax.dot_general(
        rows[...], left, (((1,), (1,)), ((), ())), preferred_element_type=F32
    ).astype(BF16)
    sums = jnp.dot(left, right, preferred_element_type=F32)
    pack(sums, False, out)


def add_kernel(got, out):
    parts = []
    for zl in range(4):
        total = got[zl * 4].astype(F32)
        for zh in range(1, 4):
            total += got[zl * 4 + zh].astype(F32)
        rest = jnp.concatenate([total[64:72, g * 32 : (g + 1) * 32] for g in range(4)], axis=0)
        parts.append(jnp.concatenate([total[:32], total[32:64], rest], axis=1))
    out[...] = jnp.concatenate(parts, axis=1).astype(BF16)


def call(kernel, name, *shapes):
    out = [jax.ShapeDtypeStruct(s, BF16) for s in shapes]
    return pl.pallas_call(
        kernel,
        out_shape=out if len(out) > 1 else out[0],
        name=name,
        compiler_params=pltpu.CompilerParams(vmem_limit_bytes=32 * 1024 * 1024),
    )


def per_device(
    pair_input,
    pair_mask,
    out_norm_gain,
    out_w_in,
    out_final_gain,
    out_w_out,
    in_norm_gain,
    in_w_in,
    in_final_gain,
    in_w_out,
):
    out_norm_gain, out_final_gain, in_norm_gain, in_final_gain = (
        g.reshape(1, WIDTH) for g in (out_norm_gain, out_final_gain, in_norm_gain, in_final_gain)
    )
    by_row = np.arange(N).reshape(ROWS, 32).T.reshape(-1)
    by_place = np.arange(N).reshape(32, ROWS).T.reshape(-1)
    out_senders = jnp.asarray(one_hot(sender_order(("x", "zl", "y", "core"))), BF16)
    in_senders = jnp.asarray(one_hot(sender_order(("x", "zl", "y", "core"))), BF16)
    out_rows = jnp.asarray(one_hot(by_row), BF16)
    in_rows = jnp.asarray(one_hot(by_place), BF16)

    mask = jnp.pad(pair_mask.astype(BF16), ((0, 16 - ROWS), (0, WIDTH - COLS)))
    pair = jnp.concatenate([pair_input.reshape(TILE, WIDTH), mask], axis=0)
    swap = [(zl * 4 + zh, zh * 4 + zl) for zl in range(4) for zh in range(4)]

    def spread(sent):
        return lax.all_to_all(sent, CHANNEL, 0, 0, tiled=True)

    def collect(pieces):
        got = lax.all_to_all(pieces, LINE, 0, 0, tiled=True)
        sums = call(add_kernel, "add_parts", (32, 4 * TILE))(got)
        return lax.all_to_all(sums, PLANE, 0, 0, tiled=True)

    swapped_pair = lax.ppermute(pair, LINE, swap)
    sent = call(first_kernel, "project_first", (WIDTH, 2 * TILE))(pair, out_norm_gain, out_w_in)
    pieces = call(outgoing_kernel, "outgoing", (16, 72, 128))(spread(sent), out_senders, out_rows)
    tri = collect(pieces)
    swapped_middle, sent = call(middle_kernel, "middle", (TILE, WIDTH), (WIDTH, 2 * TILE))(
        swapped_pair, tri, out_norm_gain, out_w_in, out_final_gain, out_w_out, in_norm_gain, in_w_in
    )
    middle = lax.ppermute(swapped_middle, LINE, swap)
    pieces = call(incoming_kernel, "incoming", (16, 72, 128))(spread(sent), in_senders, in_rows)
    tri = collect(pieces)
    out = call(last_kernel, "last", (TILE, WIDTH))(
        middle, tri, in_norm_gain, in_w_in, in_final_gain, in_w_out
    )
    return out.reshape(ROWS, COLS, WIDTH)


def solution(mesh):
    fine = Mesh(
        mesh.devices.reshape([SIZES[a] for a in ROW + COL]), ROW + COL
    )
    placed = (P(ROW, COL, None), P(ROW, COL), P(), P(), P(), P(), P(), P(), P(), P())
    return jax.shard_map(
        per_device, mesh=fine, in_specs=placed, out_specs=P(ROW, COL, None), check_vma=False
    )
```

```python
import jax
import jax.numpy as jnp
import numpy as np
from jax import lax
from jax.experimental import pallas as pl
from jax.experimental.pallas import tpu as pltpu
from jax.sharding import Mesh
from jax.sharding import PartitionSpec as P

ROW = ("zl", "y", "core")
COL = ("x", "zh")
SIZES = {"zl": 4, "y": 4, "core": 2, "x": 4, "zh": 4}
CHANNEL = ("y", "zh", "zl", "core")
PLANE = ("x", "y")
LINE = ("zh", "zl", "core")

ROWS, COLS, WIDTH = 12, 24, 128
TILE = ROWS * COLS
N = 384
F32, BF16 = jnp.float32, jnp.bfloat16


def one_hot(places):
    table = np.zeros((len(places), len(places)), np.float32)
    table[np.arange(len(places)), places] = 1
    return table


def sender_order(names):
    index = np.arange(128).reshape([SIZES[a] for a in CHANNEL])
    return index.transpose([CHANNEL.index(a) for a in names]).reshape(-1)


def layer_norm(values, gain):
    center = values - jnp.mean(values, axis=-1, keepdims=True)
    spread = jnp.mean(center * center, axis=-1, keepdims=True)
    return center * lax.rsqrt(spread + 1e-05) * gain


def flat_mask(mask):
    return jnp.concatenate([mask[i : i + 1] for i in range(ROWS)], axis=1)


def project(normed, mask, w_in):
    proj = lax.dot_general(
        w_in[:, : 4 * WIDTH], normed, (((0,), (1,)), ((), ())), preferred_element_type=F32
    )
    left = proj[:WIDTH] * jax.nn.sigmoid(proj[2 * WIDTH : 3 * WIDTH]) * mask
    right = proj[WIDTH : 2 * WIDTH] * jax.nn.sigmoid(proj[3 * WIDTH : 4 * WIDTH]) * mask
    return jnp.concatenate([left, right], axis=1).astype(BF16)


def update(pair, tri, norm_gain, w_in, final_gain, w_out):
    tri = tri.astype(F32)
    tri = jnp.concatenate([tri[:, i * TILE : (i + 1) * TILE] for i in range(4)], axis=0)
    final = layer_norm(tri.T, final_gain).astype(BF16)
    normed = layer_norm(pair, norm_gain).astype(BF16)
    gate = jax.nn.sigmoid(jnp.dot(normed, w_in[:, 4 * WIDTH :], preferred_element_type=F32))
    return (pair + jnp.dot(final, w_out, preferred_element_type=F32) * gate).astype(BF16)


def first_kernel(pair_ref, norm_gain, w_in, sent):
    pair = pair_ref[:TILE].astype(F32)
    mask = flat_mask(pair_ref[TILE : TILE + 16, :].astype(F32)[:ROWS, :COLS])
    normed = layer_norm(pair, norm_gain[...]).astype(BF16)
    sent[...] = project(normed, mask, w_in)


def middle_kernel(
    pair_ref, tri, norm_gain, w_in, final_gain, w_out, next_gain, next_w_in, middle, sent
):
    pair = pair_ref[:TILE].astype(F32)
    mask = flat_mask(pair_ref[TILE : TILE + 16, :].astype(F32)[:ROWS, :COLS])
    new = update(pair, tri[...], norm_gain[...], w_in, final_gain[...], w_out[...])
    middle[...] = new
    normed = layer_norm(new.astype(F32), next_gain[...]).astype(BF16)
    sent[...] = project(normed, mask, next_w_in)


def last_kernel(pair_ref, tri, norm_gain, w_in, final_gain, w_out, out):
    pair = pair_ref[...].astype(F32)
    out[...] = update(pair, tri[...], norm_gain[...], w_in, final_gain[...], w_out[...])


def pack(sums, swapped, out):
    for x in range(4):
        strips = []
        for zh in range(4):
            at = (x * 4 + zh) * COLS
            strips.append(
                jnp.concatenate(
                    [sums[i * 32 : (i + 1) * 32, at : at + COLS] for i in range(ROWS)], axis=1
                )
            )
        for y in range(4):
            piece = jnp.concatenate([s[y * 8 : (y + 1) * 8] for s in strips], axis=0)
            rest = jnp.concatenate([piece[g * 8 : (g + 1) * 8, 256:] for g in range(4)], axis=1)
            place = y * 4 + x if swapped else x * 4 + y
            out[place] = jnp.concatenate([piece[:, :128], piece[:, 128:256], rest], axis=0).astype(BF16)


def outgoing_kernel(got, senders, rows, out):
    got = jnp.dot(senders[...], got[...], preferred_element_type=F32)

    def operand(at):
        return jnp.concatenate(
            [
                jnp.concatenate(
                    [got[g * 32 : (g + 1) * 32, at + i * COLS : at + (i + 1) * COLS] for g in range(4)],
                    axis=1,
                )
                for i in range(ROWS)
            ],
            axis=0,
        ).astype(BF16)

    left, right = operand(0), operand(TILE)
    right = jnp.dot(rows[...], right, preferred_element_type=F32).astype(BF16)
    sums = lax.dot_general(left, right, (((1,), (1,)), ((), ())), preferred_element_type=F32)
    pack(sums, True, out)


def incoming_kernel(got, rows, out):
    got = got[...].astype(F32)

    def operand(at):
        return jnp.concatenate(
            [
                jnp.concatenate(
                    [got[g * 8 : (g + 1) * 8, at + k * COLS : at + (k + 1) * COLS] for g in range(16)],
                    axis=1,
                )
                for k in range(ROWS)
            ],
            axis=0,
        ).astype(BF16)

    left, right = operand(0), operand(TILE)
    left = lax.dot_general(
        rows[...], left, (((1,), (1,)), ((), ())), preferred_element_type=F32
    ).astype(BF16)
    sums = jnp.dot(left, right, preferred_element_type=F32)
    pack(sums, False, out)


def add_kernel(got, out):
    parts = []
    for y in range(4):
        total = got[y].astype(F32)
        for x in range(1, 4):
            total += got[x * 4 + y].astype(F32)
        rest = jnp.concatenate([total[64:72, g * 32 : (g + 1) * 32] for g in range(4)], axis=0)
        parts.append(jnp.concatenate([total[:32], total[32:64], rest], axis=1))
    out[...] = jnp.concatenate(parts, axis=1).astype(BF16)


def call(kernel, name, *shapes):
    out = [jax.ShapeDtypeStruct(s, BF16) for s in shapes]
    return pl.pallas_call(
        kernel,
        out_shape=out if len(out) > 1 else out[0],
        name=name,
        compiler_params=pltpu.CompilerParams(vmem_limit_bytes=32 * 1024 * 1024),
    )


def per_device(
    pair_input,
    pair_mask,
    out_norm_gain,
    out_w_in,
    out_final_gain,
    out_w_out,
    in_norm_gain,
    in_w_in,
    in_final_gain,
    in_w_out,
):
    out_norm_gain, out_final_gain, in_norm_gain, in_final_gain = (
        g.reshape(1, WIDTH) for g in (out_norm_gain, out_final_gain, in_norm_gain, in_final_gain)
    )
    by_array = np.arange(N).reshape(ROWS, 4, 4, 2).transpose(2, 1, 3, 0).reshape(-1)
    by_place = np.arange(N).reshape(4, 4, 2, ROWS).transpose(3, 1, 0, 2).reshape(-1)
    out_senders = jnp.asarray(one_hot(sender_order(("zh", "y", "zl", "core"))), BF16)
    out_rows = jnp.asarray(one_hot(by_array), BF16)
    in_rows = jnp.asarray(one_hot(by_place), BF16)

    mask = jnp.pad(pair_mask.astype(BF16), ((0, 16 - ROWS), (0, WIDTH - COLS)))
    pair = jnp.concatenate([pair_input.reshape(TILE, WIDTH), mask], axis=0)
    swap = [(x * 4 + y, y * 4 + x) for x in range(4) for y in range(4)]

    def spread(sent):
        return lax.all_to_all(sent, CHANNEL, 0, 0, tiled=True)

    def collect(pieces):
        got = lax.all_to_all(pieces, PLANE, 0, 0, tiled=True)
        sums = call(add_kernel, "add_parts", (32, 4 * TILE))(got)
        return lax.all_to_all(sums, LINE, 0, 0, tiled=True)

    swapped_pair = lax.ppermute(pair, ("y", "x"), swap)
    sent = call(first_kernel, "project_first", (WIDTH, 2 * TILE))(pair, out_norm_gain, out_w_in)
    pieces = call(outgoing_kernel, "outgoing", (16, 72, 128))(spread(sent), out_senders, out_rows)
    tri = collect(pieces)
    swapped_middle, sent = call(middle_kernel, "middle", (TILE, WIDTH), (WIDTH, 2 * TILE))(
        swapped_pair, tri, out_norm_gain, out_w_in, out_final_gain, out_w_out, in_norm_gain, in_w_in
    )
    middle = lax.ppermute(swapped_middle, ("y", "x"), swap)
    pieces = call(incoming_kernel, "incoming", (16, 72, 128))(spread(sent), in_rows)
    tri = collect(pieces)
    out = call(last_kernel, "last", (TILE, WIDTH))(
        middle, tri, in_norm_gain, in_w_in, in_final_gain, in_w_out
    )
    return out.reshape(ROWS, COLS, WIDTH)


def solution(mesh):
    fine = Mesh(
        mesh.devices.reshape([SIZES[a] for a in ROW + COL]), ROW + COL
    )
    placed = (P(ROW, COL, None), P(ROW, COL), P(), P(), P(), P(), P(), P(), P(), P())
    return jax.shard_map(
        per_device, mesh=fine, in_specs=placed, out_specs=P(ROW, COL, None), check_vma=False
    )
```

```python
import jax
import jax.numpy as jnp
import numpy as np
from jax import lax
from jax.experimental import pallas as pl
from jax.experimental.pallas import tpu as pltpu
from jax.sharding import Mesh
from jax.sharding import PartitionSpec as P

ROW = ("zl", "y", "core")
COL = ("x", "zh")
SIZES = {"zl": 4, "y": 4, "core": 2, "x": 4, "zh": 4}
CHANNEL = ("zl", "x", "y", "core")
LINE = ("zh", "zl")
PLANE = ("x", "y", "core")

ROWS, COLS, WIDTH = 12, 24, 128
TILE = ROWS * COLS
N = 384
F32, BF16 = jnp.float32, jnp.bfloat16


def one_hot(places):
    table = np.zeros((len(places), len(places)), np.float32)
    table[np.arange(len(places)), places] = 1
    return table


def sender_order(names):
    index = np.arange(128).reshape([SIZES[a] for a in CHANNEL])
    return index.transpose([CHANNEL.index(a) for a in names]).reshape(-1)


def layer_norm(values, gain):
    center = values - jnp.mean(values, axis=-1, keepdims=True)
    spread = jnp.mean(center * center, axis=-1, keepdims=True)
    return center * lax.rsqrt(spread + 1e-05) * gain


def flat_mask(mask):
    return jnp.concatenate([mask[i : i + 1] for i in range(ROWS)], axis=1)


def project(normed, mask, w_in):
    proj = lax.dot_general(
        w_in[:, : 4 * WIDTH], normed, (((0,), (1,)), ((), ())), preferred_element_type=F32
    )
    left = proj[:WIDTH] * jax.nn.sigmoid(proj[2 * WIDTH : 3 * WIDTH]) * mask
    right = proj[WIDTH : 2 * WIDTH] * jax.nn.sigmoid(proj[3 * WIDTH : 4 * WIDTH]) * mask
    return left.astype(BF16), right.astype(BF16)


def update(pair, tri, norm_gain, w_in, final_gain, w_out):
    tri = jnp.concatenate(tri, axis=0)
    final = layer_norm(tri.T, final_gain).astype(BF16)
    normed = layer_norm(pair, norm_gain).astype(BF16)
    gate = jax.nn.sigmoid(jnp.dot(normed, w_in[:, 4 * WIDTH :], preferred_element_type=F32))
    return (pair + jnp.dot(final, w_out, preferred_element_type=F32) * gate).astype(BF16)


def sums_of(tri):
    rows = [tri[:, i, :].astype(F32) for i in range(2)]
    return [r[:, i * TILE : (i + 1) * TILE] for r in rows for i in range(2)]


def first_kernel(pair_ref, mask_ref, norm_gain, w_in, kept, sent):
    pair = pair_ref[...]
    mask = mask_ref[...].astype(F32)
    kept[:TILE] = pair
    wide = jnp.concatenate([mask, jnp.zeros((ROWS, WIDTH - COLS), F32)], axis=1)
    kept[TILE:] = jnp.concatenate([wide, jnp.zeros((16 - ROWS, WIDTH), F32)], axis=0).astype(BF16)
    normed = layer_norm(pair.astype(F32), norm_gain[...]).astype(BF16)
    sent[:, 0, :], sent[:, 1, :] = project(normed, flat_mask(mask), w_in)


def middle_kernel(
    pair_ref, tri, norm_gain, w_in, final_gain, w_out, next_gain, next_w_in, middle, sent
):
    pair = pair_ref[:TILE].astype(F32)
    mask = flat_mask(pair_ref[TILE : TILE + 16, :].astype(F32)[:ROWS, :COLS])
    new = update(pair, sums_of(tri), norm_gain[...], w_in, final_gain[...], w_out[...])
    middle[...] = new
    normed = layer_norm(new.astype(F32), next_gain[...]).astype(BF16)
    sent[:, 0, :], sent[:, 1, :] = project(normed, mask, next_w_in)


def last_kernel(pair_ref, tri, norm_gain, w_in, final_gain, w_out, out):
    pair = pair_ref[...].astype(F32)
    out[...] = update(pair, sums_of(tri), norm_gain[...], w_in, final_gain[...], w_out[...])


def pack(sums, swapped, out):
    for zh in range(4):
        strips = []
        for x in range(4):
            at = (x * 4 + zh) * COLS
            strips.append(
                jnp.concatenate(
                    [sums[i * 32 : (i + 1) * 32, at : at + COLS] for i in range(ROWS)], axis=1
                )
            )
        for zl in range(4):
            piece = jnp.concatenate([s[zl * 8 : (zl + 1) * 8] for s in strips], axis=0)
            rest = jnp.concatenate([piece[g * 8 : (g + 1) * 8, 256:] for g in range(4)], axis=1)
            place = zl * 4 + zh if swapped else zh * 4 + zl
            out[place] = jnp.concatenate([piece[:, :128], piece[:, 128:256], rest], axis=0).astype(BF16)


def outgoing_kernel(got, senders, rows, moved, out):
    sides = [jnp.dot(senders[...], got[:, i, :], preferred_element_type=F32) for i in range(2)]

    def operand(got):
        return jnp.concatenate(
            [
                jnp.concatenate(
                    [got[x * 32 : (x + 1) * 32, i * COLS : (i + 1) * COLS] for x in range(4)],
                    axis=1,
                )
                for i in range(ROWS)
            ],
            axis=0,
        ).astype(BF16)

    left, right = operand(sides[0]), operand(sides[1])
    right = jnp.dot(rows[...], right, preferred_element_type=F32).astype(BF16)
    sums = lax.dot_general(left, right, (((1,), (1,)), ((), ())), preferred_element_type=F32)
    pack(sums, True, out)


def incoming_kernel(got, senders, rows, moved, out):
    sides = [jnp.dot(senders[...], got[:, i, :], preferred_element_type=F32) for i in range(2)]

    def operand(got):
        return jnp.concatenate(
            [
                jnp.concatenate(
                    [got[g * 8 : (g + 1) * 8, k * COLS : (k + 1) * COLS] for g in range(16)],
                    axis=1,
                )
                for k in range(ROWS)
            ],
            axis=0,
        ).astype(BF16)

    left, right = operand(sides[0]), operand(sides[1])
    left = lax.dot_general(
        rows[...], left, (((1,), (1,)), ((), ())), preferred_element_type=F32
    ).astype(BF16)
    sums = jnp.dot(left, right, preferred_element_type=F32)
    pack(sums, False, out)


def add_kernel(got, out):
    parts = []
    for zl in range(4):
        total = got[zl].astype(F32)
        for zh in range(1, 4):
            total += got[zh * 4 + zl].astype(F32)
        rest = jnp.concatenate([total[64:72, g * 32 : (g + 1) * 32] for g in range(4)], axis=0)
        parts.append(jnp.concatenate([total[:32], total[32:64], rest], axis=1))
    for i in range(2):
        out[:, i, :] = jnp.concatenate(parts[2 * i : 2 * i + 2], axis=1).astype(BF16)


def call(kernel, name, n_in, *shapes, unread=False):
    out = [jax.ShapeDtypeStruct(s, BF16) for s in shapes]
    specs = [pl.BlockSpec(memory_space=pltpu.VMEM)] * n_in
    if unread:
        specs[-1] = pl.BlockSpec(memory_space=pl.ANY)
    return pl.pallas_call(
        kernel,
        in_specs=specs,
        out_shape=out if len(out) > 1 else out[0],
        name=name,
        compiler_params=pltpu.CompilerParams(vmem_limit_bytes=32 * 1024 * 1024),
    )


def per_device(
    pair_input,
    pair_mask,
    out_norm_gain,
    out_w_in,
    out_final_gain,
    out_w_out,
    in_norm_gain,
    in_w_in,
    in_final_gain,
    in_w_out,
):
    out_norm_gain, out_final_gain, in_norm_gain, in_final_gain = (
        g.reshape(1, WIDTH) for g in (out_norm_gain, out_final_gain, in_norm_gain, in_final_gain)
    )
    by_row = np.arange(N).reshape(ROWS, 32).T.reshape(-1)
    by_place = np.arange(N).reshape(32, ROWS).T.reshape(-1)
    out_senders = jnp.asarray(one_hot(sender_order(("x", "zl", "y", "core"))), BF16)
    in_senders = jnp.asarray(one_hot(sender_order(("x", "zl", "y", "core"))), BF16)
    out_rows = jnp.asarray(one_hot(by_row), BF16)
    in_rows = jnp.asarray(one_hot(by_place), BF16)

    swap = [(zl * 4 + zh, zh * 4 + zl) for zl in range(4) for zh in range(4)]

    def spread(sent):
        return lax.all_to_all(sent, CHANNEL, 0, 0, tiled=True)

    def collect(pieces):
        got = lax.all_to_all(pieces, LINE, 0, 0, tiled=True)
        sums = call(add_kernel, "add_parts", 1, (32, 2, 2 * TILE))(got)
        return lax.all_to_all(sums, PLANE, 0, 0, tiled=True)

    pair, sent = call(
        first_kernel, "project_first", 4, (TILE + 16, WIDTH), (WIDTH, 2, TILE)
    )(pair_input.reshape(TILE, WIDTH), pair_mask, out_norm_gain, out_w_in)
    swapped_pair = lax.ppermute(pair, ("zl", "zh"), swap)
    pieces = call(outgoing_kernel, "outgoing", 4, (16, 72, 128), unread=True)(
        spread(sent), out_senders, out_rows, swapped_pair
    )
    swapped_middle, sent = call(middle_kernel, "middle", 8, (TILE, WIDTH), (WIDTH, 2, TILE))(
        swapped_pair, collect(pieces), out_norm_gain, out_w_in, out_final_gain, out_w_out, in_norm_gain, in_w_in
    )
    middle = lax.ppermute(swapped_middle, ("zl", "zh"), swap)
    pieces = call(incoming_kernel, "incoming", 4, (16, 72, 128), unread=True)(
        spread(sent), in_senders, in_rows, middle
    )
    out = call(last_kernel, "last", 6, (TILE, WIDTH))(
        middle, collect(pieces), in_norm_gain, in_w_in, in_final_gain, in_w_out
    )
    return out.reshape(ROWS, COLS, WIDTH)


def solution(mesh):
    fine = Mesh(
        mesh.devices.reshape([SIZES[a] for a in ROW + COL]), ROW + COL
    )
    placed = (P(ROW, COL, None), P(ROW, COL), P(), P(), P(), P(), P(), P(), P(), P())
    return jax.shard_map(
        per_device, mesh=fine, in_specs=placed, out_specs=P(ROW, COL, None), check_vma=False
    )
```

```python
import jax
import jax.numpy as jnp
import numpy as np
from jax import lax
from jax.experimental import pallas as pl
from jax.experimental.pallas import tpu as pltpu
from jax.sharding import Mesh
from jax.sharding import PartitionSpec as P

ROW = ("zl", "y", "core")
COL = ("x", "zh")
SIZES = {"zl": 4, "y": 4, "core": 2, "x": 4, "zh": 4}
OUT_CHANNEL = ("zl", "x", "y", "core")
IN_CHANNEL = ("x", "y", "zl", "core")
LINE = ("zl", "zh")
PLANE = ("x", "y", "core")

ROWS, COLS, WIDTH = 12, 24, 128
TILE = ROWS * COLS
N = 384
F32, BF16 = jnp.float32, jnp.bfloat16


def one_hot(places):
    table = np.zeros((len(places), len(places)), np.float32)
    table[np.arange(len(places)), places] = 1
    return table


def sender_order(names):
    index = np.arange(128).reshape([SIZES[a] for a in OUT_CHANNEL])
    return index.transpose([OUT_CHANNEL.index(a) for a in names]).reshape(-1)


def layer_norm(values, gain):
    center = values - jnp.mean(values, axis=-1, keepdims=True)
    spread = jnp.mean(center * center, axis=-1, keepdims=True)
    return center * lax.rsqrt(spread + 1e-05) * gain


def flat_mask(mask):
    return jnp.concatenate([mask[i : i + 1] for i in range(ROWS)], axis=1)


def project(normed, mask, w_in):
    proj = lax.dot_general(
        w_in[:, : 4 * WIDTH], normed, (((0,), (1,)), ((), ())), preferred_element_type=F32
    )
    left = proj[:WIDTH] * jax.nn.sigmoid(proj[2 * WIDTH : 3 * WIDTH]) * mask
    right = proj[WIDTH : 2 * WIDTH] * jax.nn.sigmoid(proj[3 * WIDTH : 4 * WIDTH]) * mask
    return left.astype(BF16), right.astype(BF16)


def update(pair, tri, norm_gain, w_in, final_gain, w_out):
    final = layer_norm(tri.T, final_gain).astype(BF16)
    normed = layer_norm(pair, norm_gain).astype(BF16)
    gate = jax.nn.sigmoid(jnp.dot(normed, w_in[:, 4 * WIDTH :], preferred_element_type=F32))
    return (pair + jnp.dot(final, w_out, preferred_element_type=F32) * gate).astype(BF16)


def sums_of(tri):
    rows = [tri[:, i, :].astype(F32) for i in range(2)]
    return jnp.concatenate([r[:, i * TILE : (i + 1) * TILE] for r in rows for i in range(2)], axis=0)


def first_kernel(pair_ref, mask_ref, g0, g1, g2, g3, w_in, sent, gains, pair, mask, weights, sems):
    copies = [
        pltpu.make_async_copy(pair_ref, pair, sems.at[0]),
        pltpu.make_async_copy(mask_ref, mask, sems.at[1]),
        pltpu.make_async_copy(w_in.at[:, pl.ds(0, 4 * WIDTH)], weights, sems.at[2]),
    ]
    for i, gain in enumerate((g0, g1, g2, g3)):
        copies.append(pltpu.make_async_copy(gain, gains.at[pl.ds(i, 1)], sems.at[3 + i]))
    for copy in copies:
        copy.start()
    for copy in copies:
        copy.wait()
    normed = layer_norm(pair[...].astype(F32), gains[0:1]).astype(BF16)
    sent[:, 0, :], sent[:, 1, :] = project(normed, flat_mask(mask[...].astype(F32)), weights[...])


def middle_kernel(pair_ref, mask, tri, gains, w_in, w_out, next_w_in, middle, sent):
    pair = pair_ref[...].astype(F32)
    new = update(pair, sums_of(tri), gains[0:1], w_in, gains[1:2], w_out[...])
    middle[...] = new
    normed = layer_norm(new.astype(F32), gains[2:3]).astype(BF16)
    sent[:, 0, :], sent[:, 1, :] = project(normed, flat_mask(mask[...].astype(F32)), next_w_in)


def last_kernel(pair_ref, tri, gains, w_in, w_out, out):
    pair = pair_ref[...].astype(F32)
    sums = jnp.concatenate([tri[:, half, :].astype(F32) for half in range(2)], axis=1)
    out[...] = update(pair, sums, gains[2:3], w_in, gains[3:4], w_out[...])


def pack(sums, out):
    for zh in range(4):
        strips = []
        for x in range(4):
            at = (x * 4 + zh) * COLS
            strips.append(
                jnp.concatenate(
                    [sums[i * 32 : (i + 1) * 32, at : at + COLS] for i in range(ROWS)], axis=1
                )
            )
        for zl in range(4):
            piece = jnp.concatenate([s[zl * 8 : (zl + 1) * 8] for s in strips], axis=0)
            rest = jnp.concatenate([piece[g * 8 : (g + 1) * 8, 256:] for g in range(4)], axis=1)
            out[zl * 4 + zh] = jnp.concatenate([piece[:, :128], piece[:, 128:256], rest], axis=0).astype(BF16)


def outgoing_kernel(got, senders, rows, out):
    sides = [jnp.dot(senders[...], got[:, i, :], preferred_element_type=F32) for i in range(2)]

    def operand(got):
        return jnp.concatenate(
            [
                jnp.concatenate(
                    [got[x * 32 : (x + 1) * 32, i * COLS : (i + 1) * COLS] for x in range(4)],
                    axis=1,
                )
                for i in range(ROWS)
            ],
            axis=0,
        ).astype(BF16)

    left, right = operand(sides[0]), operand(sides[1])
    right = jnp.dot(rows[...], right, preferred_element_type=F32).astype(BF16)
    sums = lax.dot_general(left, right, (((1,), (1,)), ((), ())), preferred_element_type=F32)
    pack(sums, out)


def split_kernel(got, left):
    side = got[:, 0, :].astype(F32)
    rest = jnp.concatenate([side[g * 32 : (g + 1) * 32, 256:] for g in range(4)], axis=1)
    left[...] = jnp.concatenate([side[:, :128], side[:, 128:256], rest], axis=0).astype(BF16)


def incoming_kernel(got, lefts, rows, out):
    def operand(side):
        return jnp.concatenate(
            [
                jnp.concatenate(
                    [side[x * 32 : (x + 1) * 32, k * COLS : (k + 1) * COLS] for x in range(4)], axis=1
                )
                for k in range(ROWS)
            ],
            axis=0,
        ).astype(BF16)

    right = operand(got[:, 1, :].astype(F32))
    for zh in range(4):
        left = lefts[zh].astype(F32)
        rest = jnp.concatenate([left[256:, g * 32 : (g + 1) * 32] for g in range(4)], axis=0)
        left = operand(jnp.concatenate([left[:128], left[128:256], rest], axis=1))
        left = lax.dot_general(
            rows[...], left, (((1,), (1,)), ((), ())), preferred_element_type=F32
        ).astype(BF16)
        sums = jnp.dot(left, right, preferred_element_type=F32)
        for x in range(4):
            piece = [sums[i * 8 : (i + 1) * 8, x * COLS : (x + 1) * COLS] for i in range(ROWS)]
            at = x * 32 + zh * 8
            for half in range(2):
                part = jnp.concatenate(piece[half * 6 : half * 6 + 6], axis=1)
                out[at : at + 8, half, :] = part.astype(BF16)


def add_kernel(got, out):
    parts = []
    for zl in range(4):
        total = got[zl * 4].astype(F32)
        for zh in range(1, 4):
            total += got[zl * 4 + zh].astype(F32)
        rest = jnp.concatenate([total[64:72, g * 32 : (g + 1) * 32] for g in range(4)], axis=0)
        parts.append(jnp.concatenate([total[:32], total[32:64], rest], axis=1))
    for i in range(2):
        out[:, i, :] = jnp.concatenate(parts[2 * i : 2 * i + 2], axis=1).astype(BF16)


def call(kernel, name, *shapes):
    out = [jax.ShapeDtypeStruct(s, BF16) for s in shapes]
    return pl.pallas_call(
        kernel,
        out_shape=out if len(out) > 1 else out[0],
        name=name,
        compiler_params=pltpu.CompilerParams(vmem_limit_bytes=32 * 1024 * 1024),
    )


def call_first(*operands):
    return pl.pallas_call(
        first_kernel,
        in_specs=[pl.BlockSpec(memory_space=pltpu.HBM)] * len(operands),
        out_shape=[
            jax.ShapeDtypeStruct((WIDTH, 2, TILE), BF16),
            jax.ShapeDtypeStruct((4, WIDTH), F32),
        ],
        scratch_shapes=[
            pltpu.VMEM((TILE, WIDTH), BF16),
            pltpu.VMEM((ROWS, COLS), jnp.int32),
            pltpu.VMEM((WIDTH, 4 * WIDTH), BF16),
            pltpu.SemaphoreType.DMA((7,)),
        ],
        name="project_first",
        compiler_params=pltpu.CompilerParams(vmem_limit_bytes=60 * 1024 * 1024),
    )(*operands)


def gather_lefts(left):
    return lax.all_gather(left, "zh")


def per_device(
    pair_input,
    pair_mask,
    out_norm_gain,
    out_w_in,
    out_final_gain,
    out_w_out,
    in_norm_gain,
    in_w_in,
    in_final_gain,
    in_w_out,
):
    out_norm_gain, out_final_gain, in_norm_gain, in_final_gain = (
        g.reshape(1, WIDTH) for g in (out_norm_gain, out_final_gain, in_norm_gain, in_final_gain)
    )
    by_row = np.arange(N).reshape(ROWS, 32).T.reshape(-1)
    by_place = np.arange(96).reshape(8, ROWS).T.reshape(-1)
    out_senders = jnp.asarray(one_hot(sender_order(("x", "zl", "y", "core"))), BF16)
    out_rows = jnp.asarray(one_hot(by_row), BF16)
    in_rows = jnp.asarray(one_hot(by_place), BF16)

    pair = pair_input.reshape(TILE, WIDTH)
    sent, gains = call_first(
        pair,
        pair_mask,
        out_norm_gain,
        out_final_gain,
        in_norm_gain,
        in_final_gain,
        out_w_in,
    )
    got = lax.all_to_all(sent, OUT_CHANNEL, 0, 0, tiled=True)
    pieces = call(outgoing_kernel, "outgoing", (16, 72, 128))(got, out_senders, out_rows)
    got = lax.all_to_all(pieces, LINE, 0, 0, tiled=True)
    sums = call(add_kernel, "add_parts", (32, 2, 2 * TILE))(got)
    tri = lax.all_to_all(sums, PLANE, 0, 0, tiled=True)

    middle, sent = call(middle_kernel, "middle", (TILE, WIDTH), (WIDTH, 2, TILE))(
        pair, pair_mask, tri, gains, out_w_in, out_w_out, in_w_in
    )
    got = lax.all_to_all(sent, IN_CHANNEL, 0, 0, tiled=True)
    left = call(split_kernel, "split", (TILE, WIDTH))(got)
    lefts = gather_lefts(left)
    sums = call(incoming_kernel, "incoming", (WIDTH, 2, TILE // 2))(got, lefts, in_rows)
    tri = lax.all_to_all(sums, IN_CHANNEL, 0, 0, tiled=True)
    out = call(last_kernel, "last", (TILE, WIDTH))(middle, tri, gains, in_w_in, in_w_out)
    return out.reshape(ROWS, COLS, WIDTH)


def solution(mesh):
    fine = Mesh(
        mesh.devices.reshape([SIZES[a] for a in ROW + COL]), ROW + COL
    )
    placed = (P(ROW, COL, None), P(ROW, COL), P(), P(), P(), P(), P(), P(), P(), P())
    return jax.shard_map(
        per_device, mesh=fine, in_specs=placed, out_specs=P(ROW, COL, None), check_vma=False
    )
```

```python
import jax
import jax.numpy as jnp
import ml_dtypes
import numpy as np
from jax import lax
from jax.experimental import pallas as pl
from jax.experimental.pallas import tpu as pltpu
from jax.sharding import Mesh
from jax.sharding import PartitionSpec as P

ROW = ("zl", "y", "core")
COL = ("x", "zh")
SIZES = {"zl": 4, "y": 4, "core": 2, "x": 4, "zh": 4}
OUT_CHANNEL = ("zl", "x", "y")
IN_CHANNEL = ("x", "y", "zl")
LINE = ("zl", "zh")
PLANE = ("x", "y")

ROWS, COLS, WIDTH = 12, 24, 128
TILE = ROWS * COLS
PAIRS = WIDTH // 2
N = 384
F32, BF16 = jnp.float32, jnp.bfloat16


def one_hot(places, width=None):
    places = np.asarray(places).reshape(-1)
    table = np.zeros((len(places), width or len(places)), np.float32)
    table[np.arange(len(places))[places >= 0], places[places >= 0]] = 1
    return table.astype(ml_dtypes.bfloat16)


def reorder(sizes, order):
    return np.arange(np.prod(sizes)).reshape(sizes).transpose(order)


def layer_norm(values, gain):
    center = values - jnp.mean(values, axis=-1, keepdims=True)
    spread = jnp.mean(center * center, axis=-1, keepdims=True)
    return center * lax.rsqrt(spread + 1e-05) * gain


def flat_mask(mask):
    return jnp.concatenate([mask[i : i + 1] for i in range(ROWS)], axis=1)


def project(normed, mask, w_in):
    proj = lax.dot_general(
        w_in[:, : 4 * WIDTH], normed, (((0,), (1,)), ((), ())), preferred_element_type=F32
    )
    left = proj[:WIDTH] * jax.nn.sigmoid(proj[2 * WIDTH : 3 * WIDTH]) * mask
    right = proj[WIDTH : 2 * WIDTH] * jax.nn.sigmoid(proj[3 * WIDTH : 4 * WIDTH]) * mask
    return [jnp.concatenate([v[:PAIRS], v[PAIRS:]], axis=1).astype(BF16) for v in (left, right)]


def update(pair, tri, norm_gain, w_in, final_gain, w_out):
    final = layer_norm(tri.T, final_gain).astype(BF16)
    normed = layer_norm(pair, norm_gain).astype(BF16)
    gate = jax.nn.sigmoid(jnp.dot(normed, w_in[:, 4 * WIDTH :], preferred_element_type=F32))
    return (pair + jnp.dot(final, w_out, preferred_element_type=F32) * gate).astype(BF16)


def sums_of(tri):
    pair = [tri[:, i, :].astype(F32) for i in range(2)]
    return jnp.concatenate([v[:, zl * TILE : (zl + 1) * TILE] for v in pair for zl in range(4)], axis=0)


def first_kernel(pair_ref, mask_ref, g0, g1, g2, g3, w_in, sent, gains, pair, mask, weights, sems):
    copies = [
        pltpu.make_async_copy(pair_ref, pair, sems.at[0]),
        pltpu.make_async_copy(mask_ref, mask, sems.at[1]),
        pltpu.make_async_copy(w_in.at[:, pl.ds(0, 4 * WIDTH)], weights, sems.at[2]),
    ]
    for i, gain in enumerate((g0, g1, g2, g3)):
        copies.append(pltpu.make_async_copy(gain, gains.at[pl.ds(i, 1)], sems.at[3 + i]))
    for copy in copies:
        copy.start()
    for copy in copies:
        copy.wait()
    normed = layer_norm(pair[...].astype(F32), gains[0:1]).astype(BF16)
    sent[:, 0, :], sent[:, 1, :] = project(normed, flat_mask(mask[...].astype(F32)), weights[...])


def middle_kernel(pair_ref, mask, tri, gains, w_in, w_out, next_w_in, middle, sent):
    pair = pair_ref[...].astype(F32)
    new = update(pair, sums_of(tri), gains[0:1], w_in, gains[1:2], w_out[...])
    middle[...] = new
    normed = layer_norm(new.astype(F32), gains[2:3]).astype(BF16)
    sent[:, 0, :], sent[:, 1, :] = project(normed, flat_mask(mask[...].astype(F32)), next_w_in)


def last_kernel(pair_ref, tri, gains, w_in, w_out, out):
    pair = pair_ref[...].astype(F32)
    sums = jnp.concatenate([tri[:, i, :].astype(F32) for i in range(2)], axis=0)
    out[...] = update(pair, sums, gains[2:3], w_in, gains[3:4], w_out[...])


def chunks(side, wide):
    return jnp.concatenate(
        [
            jnp.concatenate([side[x * 32 : (x + 1) * 32, i * wide : (i + 1) * wide] for x in range(4)], axis=1)
            for i in range(ROWS)
        ],
        axis=0,
    )


def fold(strip):
    n = strip.shape[0] // 4
    rest = jnp.concatenate([strip[g * n : (g + 1) * n, 256:] for g in range(4)], axis=1)
    return jnp.concatenate([strip[:, :128], strip[:, 128:256], rest], axis=0)


def unfold(folded):
    n = folded.shape[0] // 9
    rest = jnp.concatenate([folded[8 * n :, g * 32 : (g + 1) * 32] for g in range(4)], axis=0)
    return jnp.concatenate([folded[: 4 * n], folded[4 * n : 8 * n], rest], axis=1)


def outgoing_kernel(core, own, both, left_order, right_order, rows, out):
    left = own[:, 0, :].astype(F32)
    left = jnp.concatenate([left[:, :TILE], left[:, TILE:]], axis=0).astype(BF16)
    left = chunks(jnp.dot(left_order[...], left, preferred_element_type=F32), COLS)
    first = lax.broadcasted_iota(jnp.int32, left.shape, 0) % 8 < 4
    left = jnp.concatenate([jnp.where(first, left, 0.0), jnp.where(first, 0.0, left)], axis=1).astype(BF16)
    right = jnp.dot(right_order[...], both[:, 1, :], preferred_element_type=F32)
    right = jnp.concatenate([chunks(right[:, :TILE], COLS), chunks(right[:, TILE:], COLS)], axis=1)
    right = jnp.dot(rows[...], right.astype(BF16), preferred_element_type=F32).astype(BF16)
    sums = lax.dot_general(left, right, (((1,), (1,)), ((), ())), preferred_element_type=F32)
    for zh in range(4):
        strips = []
        for x in range(4):
            at = (x * 4 + zh) * COLS
            strips.append(
                jnp.concatenate([sums[i * 32 : (i + 1) * 32, at : at + COLS] for i in range(ROWS)], axis=1)
            )
        for zl in range(4):
            piece = jnp.concatenate([s[zl * 8 : (zl + 1) * 8] for s in strips], axis=0)
            out[zl * 4 + zh] = fold(piece).astype(BF16)


def add_kernel(got, order, out):
    parts = []
    for zl in range(4):
        total = got[zl * 4].astype(F32)
        for zh in range(1, 4):
            total += got[zl * 4 + zh].astype(F32)
        parts.append(unfold(total))
    total = jnp.concatenate(parts, axis=1).astype(BF16)
    total = jnp.dot(order[...], total, preferred_element_type=F32).astype(BF16)
    for i in range(2):
        out[:, i, :] = total[i * 16 : (i + 1) * 16]


def by_x(side):
    return jnp.concatenate(
        [side[c * PAIRS + x * 16 : c * PAIRS + (x + 1) * 16] for x in range(4) for c in range(2)], axis=0
    )


def split_kernel(core, both, halves, rows, left):
    side = by_x(jnp.dot(both[:, 0, :], halves[core[0]], preferred_element_type=F32))
    terms = [
        lax.dot_general(
            rows[i],
            chunks(side[:, i * TILE // 2 : (i + 1) * TILE // 2], COLS // 2).astype(BF16),
            (((1,), (1,)), ((), ())),
            preferred_element_type=F32,
        )
        for i in range(2)
    ]
    left[...] = (terms[0] + terms[1]).astype(BF16)


def incoming_kernel(both, lefts, out):
    right = by_x(both[:, 1, :].astype(F32))
    right = jnp.concatenate([chunks(right[:, :TILE], COLS), chunks(right[:, TILE:], COLS)], axis=1)
    sums = jnp.dot(lefts[...], right.astype(BF16), preferred_element_type=F32)
    first = lax.broadcasted_iota(jnp.int32, (N, 4 * COLS), 0) % 8 < 4
    sums = jnp.where(first, sums[:, : 4 * COLS], sums[:, 4 * COLS :])
    for zh in range(4):
        for x in range(4):
            piece = jnp.concatenate(
                [
                    sums[zh * 96 + i * 8 : zh * 96 + (i + 1) * 8, x * COLS : (x + 1) * COLS]
                    for i in range(ROWS)
                ],
                axis=1,
            ).astype(BF16)
            at = x * 16 + zh * 4
            for i in range(2):
                out[at : at + 4, i, :] = piece[i * 4 : (i + 1) * 4]


def call(kernel, name, n_in, *shapes, scalars=0):
    out = [jax.ShapeDtypeStruct(s, BF16) for s in shapes]
    spaces = [pltpu.SMEM] * scalars + [pltpu.VMEM] * (n_in - scalars)
    return pl.pallas_call(
        kernel,
        in_specs=[pl.BlockSpec(memory_space=space) for space in spaces],
        out_shape=out if len(out) > 1 else out[0],
        name=name,
        compiler_params=pltpu.CompilerParams(vmem_limit_bytes=32 * 1024 * 1024),
    )


def call_first(*operands):
    return pl.pallas_call(
        first_kernel,
        in_specs=[pl.BlockSpec(memory_space=pltpu.HBM)] * len(operands),
        out_shape=[
            jax.ShapeDtypeStruct((PAIRS, 2, 2 * TILE), BF16),
            jax.ShapeDtypeStruct((4, WIDTH), F32),
        ],
        scratch_shapes=[
            pltpu.VMEM((TILE, WIDTH), BF16),
            pltpu.VMEM((ROWS, COLS), jnp.int32),
            pltpu.VMEM((WIDTH, 4 * WIDTH), BF16),
            pltpu.SemaphoreType.DMA((7,)),
        ],
        name="project_first",
        compiler_params=pltpu.CompilerParams(vmem_limit_bytes=60 * 1024 * 1024),
    )(*operands)


def per_device(
    pair_input,
    pair_mask,
    out_norm_gain,
    out_w_in,
    out_final_gain,
    out_w_out,
    in_norm_gain,
    in_w_in,
    in_final_gain,
    in_w_out,
):
    out_norm_gain, out_final_gain, in_norm_gain, in_final_gain = (
        g.reshape(1, WIDTH) for g in (out_norm_gain, out_final_gain, in_norm_gain, in_final_gain)
    )
    left_order = one_hot(reorder((2, 4, 4, 4), (2, 1, 0, 3)))
    right_order = one_hot(reorder((2, 4, 4, 4), (2, 1, 3, 0)))
    out_rows = one_hot(reorder((ROWS, 32), (1, 0)))
    piece_order = one_hot(reorder((4, 2, 4), (1, 0, 2)))
    halves = np.stack(
        [one_hot(reorder((2 * ROWS, 2, ROWS), (1, 0, 2))[core], 2 * TILE).T for core in range(2)]
    )
    place = np.full((2, ROWS, 2, 4), -1)
    for i in range(2):
        place[i, :, i, :] = reorder((4, ROWS), (1, 0))
    in_rows = np.stack([one_hot(place[i], 4 * ROWS) for i in range(2)])
    left_order, right_order, out_rows, piece_order, halves, in_rows = (
        jnp.asarray(t) for t in (left_order, right_order, out_rows, piece_order, halves, in_rows)
    )
    core = lax.axis_index("core").reshape(1).astype(jnp.int32)

    def spread(sent, order):
        got = lax.all_to_all(sent, order, 0, 0, tiled=True)
        return got, lax.all_gather(got, "core", tiled=True)

    pair = pair_input.reshape(TILE, WIDTH)
    sent, gains = call_first(
        pair,
        pair_mask,
        out_norm_gain,
        out_final_gain,
        in_norm_gain,
        in_final_gain,
        out_w_in,
    )
    own, both = spread(sent, OUT_CHANNEL)
    pieces = call(outgoing_kernel, "outgoing", 6, (16, 72, 128), scalars=1)(core, own, both, left_order, right_order, out_rows)
    got = lax.all_to_all(pieces, LINE, 0, 0, tiled=True)
    sums = call(add_kernel, "add_parts", 2, (16, 2, 4 * TILE))(got, piece_order)
    tri = lax.all_to_all(sums, PLANE, 0, 0, tiled=True)

    middle, sent = call(middle_kernel, "middle", 7, (TILE, WIDTH), (PAIRS, 2, 2 * TILE))(
        pair, pair_mask, tri, gains, out_w_in, out_w_out, in_w_in
    )
    _, both = spread(sent, IN_CHANNEL)
    left = call(split_kernel, "split", 4, (96, N), scalars=1)(core, both, halves, in_rows)
    lefts = lax.all_gather(left, "zh", tiled=True)
    sums = call(incoming_kernel, "incoming", 2, (PAIRS, 2, TILE))(both, lefts)
    tri = lax.all_to_all(sums, IN_CHANNEL, 0, 0, tiled=True)
    out = call(last_kernel, "last", 5, (TILE, WIDTH))(middle, tri, gains, in_w_in, in_w_out)
    return out.reshape(ROWS, COLS, WIDTH)


def solution(mesh):
    fine = Mesh(
        mesh.devices.reshape([SIZES[a] for a in ROW + COL]), ROW + COL
    )
    placed = (P(ROW, COL, None), P(ROW, COL), P(), P(), P(), P(), P(), P(), P(), P())
    return jax.shard_map(
        per_device, mesh=fine, in_specs=placed, out_specs=P(ROW, COL, None), check_vma=False
    )
```

```python
import functools

import jax
import jax.numpy as jnp
import ml_dtypes
import numpy as np
from jax import lax
from jax.experimental import pallas as pl
from jax.experimental.pallas import tpu as pltpu
from jax.sharding import Mesh
from jax.sharding import PartitionSpec as P

ROW = ("zl", "y", "core")
COL = ("x", "zh")
SIZES = {"zl": 4, "y": 4, "core": 2, "x": 4, "zh": 4}
OUT_CHANNEL = ("y", "zl", "zh")
IN_CHANNEL = ("x", "zl", "zh")
LINE = ("zl", "zh")
PLANE = ("x", "y")

ROWS, COLS, WIDTH = 12, 24, 128
TILE = ROWS * COLS
PAIRS = WIDTH // 2
N = 384
F32, BF16 = jnp.float32, jnp.bfloat16


def one_hot(places, width=None):
    places = np.asarray(places).reshape(-1)
    table = np.zeros((len(places), width or len(places)), np.float32)
    table[np.arange(len(places))[places >= 0], places[places >= 0]] = 1
    return table.astype(ml_dtypes.bfloat16)


def reorder(sizes, order):
    return np.arange(np.prod(sizes)).reshape(sizes).transpose(order)


def layer_norm(values, gain):
    center = values - jnp.mean(values, axis=-1, keepdims=True)
    spread = jnp.mean(center * center, axis=-1, keepdims=True)
    return center * lax.rsqrt(spread + 1e-05) * gain


def flat_mask(mask):
    return jnp.concatenate([mask[i : i + 1] for i in range(ROWS)], axis=1)


def project(normed, mask, w_in):
    proj = lax.dot_general(
        w_in[:, : 4 * WIDTH], normed, (((0,), (1,)), ((), ())), preferred_element_type=F32
    )
    left = proj[:WIDTH] * jax.nn.sigmoid(proj[2 * WIDTH : 3 * WIDTH]) * mask
    right = proj[WIDTH : 2 * WIDTH] * jax.nn.sigmoid(proj[3 * WIDTH : 4 * WIDTH]) * mask
    return [jnp.concatenate([v[:PAIRS], v[PAIRS:]], axis=1).astype(BF16) for v in (left, right)]


def update(pair, tri, norm_gain, w_in, final_gain, w_out):
    final = layer_norm(tri.T, final_gain).astype(BF16)
    normed = layer_norm(pair, norm_gain).astype(BF16)
    gate = jax.nn.sigmoid(jnp.dot(normed, w_in[:, 4 * WIDTH :], preferred_element_type=F32))
    return (pair + jnp.dot(final, w_out, preferred_element_type=F32) * gate).astype(BF16)


def sums_of(tri):
    pair = [tri[:, i, :].astype(F32) for i in range(2)]
    return jnp.concatenate([v[:, i * TILE : (i + 1) * TILE] for v in pair for i in range(4)], axis=0)


def first_kernel(pair_ref, mask_ref, g0, g1, g2, g3, w_in, sent, gains, pair, mask, weights, sems):
    copies = [
        pltpu.make_async_copy(pair_ref, pair, sems.at[0]),
        pltpu.make_async_copy(mask_ref, mask, sems.at[1]),
        pltpu.make_async_copy(w_in.at[:, pl.ds(0, 4 * WIDTH)], weights, sems.at[2]),
    ]
    for i, gain in enumerate((g0, g1, g2, g3)):
        copies.append(pltpu.make_async_copy(gain, gains.at[pl.ds(i, 1)], sems.at[3 + i]))
    for copy in copies:
        copy.start()
    for copy in copies:
        copy.wait()
    normed = layer_norm(pair[...].astype(F32), gains[0:1]).astype(BF16)
    sent[:, 0, :], sent[:, 1, :] = project(normed, flat_mask(mask[...].astype(F32)), weights[...])


def middle_kernel(pair_ref, mask, tri, gains, w_in, w_out, next_w_in, middle, sent):
    pair = pair_ref[...].astype(F32)
    new = update(pair, sums_of(tri), gains[0:1], w_in, gains[1:2], w_out[...])
    middle[...] = new
    normed = layer_norm(new.astype(F32), gains[2:3]).astype(BF16)
    sent[:, 0, :], sent[:, 1, :] = project(normed, flat_mask(mask[...].astype(F32)), next_w_in)


def last_kernel(pair_ref, tri, gains, w_in, w_out, out):
    pair = pair_ref[...].astype(F32)
    out[...] = update(pair, sums_of(tri), gains[2:3], w_in, gains[3:4], w_out[...])


def chunks(side, wide):
    return jnp.concatenate(
        [
            jnp.concatenate([side[x * 32 : (x + 1) * 32, i * wide : (i + 1) * wide] for x in range(4)], axis=1)
            for i in range(ROWS)
        ],
        axis=0,
    )


def fold(strip):
    n = strip.shape[0] // 4
    rest = jnp.concatenate([strip[g * n : (g + 1) * n, 256:] for g in range(4)], axis=1)
    return jnp.concatenate([strip[:, :128], strip[:, 128:256], rest], axis=0)


def unfold(folded):
    n = folded.shape[0] // 9
    rest = jnp.concatenate([folded[8 * n :, g * 32 : (g + 1) * 32] for g in range(4)], axis=0)
    return jnp.concatenate([folded[: 4 * n], folded[4 * n : 8 * n], rest], axis=1)


def pack(sums, out):
    for x in range(4):
        strips = []
        for zh in range(4):
            at = (x * 4 + zh) * COLS
            strips.append(
                jnp.concatenate([sums[i * 32 : (i + 1) * 32, at : at + COLS] for i in range(ROWS)], axis=1)
            )
        for y in range(4):
            piece = jnp.concatenate([s[y * 8 : (y + 1) * 8] for s in strips], axis=0)
            out[x * 4 + y] = fold(piece).astype(BF16)


def outgoing_kernel(core, own, both, left_order, right_order, rows, out):
    left = own[:, 0, :].astype(F32)
    left = jnp.concatenate([left[:, :TILE], left[:, TILE:]], axis=0).astype(BF16)
    left = chunks(jnp.dot(left_order[...], left, preferred_element_type=F32), COLS)
    first = lax.broadcasted_iota(jnp.int32, left.shape, 0) % 8 < 4
    left = jnp.concatenate([jnp.where(first, left, 0.0), jnp.where(first, 0.0, left)], axis=1).astype(BF16)
    right = jnp.dot(right_order[...], both[:, 1, :], preferred_element_type=F32)
    right = jnp.concatenate([chunks(right[:, :TILE], COLS), chunks(right[:, TILE:], COLS)], axis=1)
    right = jnp.dot(rows[...], right.astype(BF16), preferred_element_type=F32).astype(BF16)
    sums = lax.dot_general(left, right, (((1,), (1,)), ((), ())), preferred_element_type=F32)
    pack(sums, out)


def incoming_kernel(core, both, order, rows, out):
    def operand(side, wide):
        return jnp.concatenate(
            [
                jnp.concatenate(
                    [side[g * 8 : (g + 1) * 8, k * COLS : k * COLS + wide] for g in range(16)], axis=1
                )
                for k in range(ROWS)
            ],
            axis=0,
        ).astype(BF16)

    left = jnp.dot(order[...], both[:, 0, :], preferred_element_type=F32)
    left = jnp.where(core[0] == 0, left, jnp.concatenate([left[:, ROWS:], left[:, :ROWS]], axis=1))
    left = [operand(left[:, i * TILE : (i + 1) * TILE], COLS // 2) for i in range(2)]
    left = [
        lax.dot_general(rows[i], left[i], (((1,), (1,)), ((), ())), preferred_element_type=F32)
        for i in range(2)
    ]
    left = jnp.concatenate(left, axis=1).astype(BF16)
    right = jnp.dot(order[...], both[:, 1, :], preferred_element_type=F32)
    right = [operand(right[:, i * TILE : (i + 1) * TILE], COLS) for i in range(2)]
    sums = jnp.dot(left, jnp.concatenate(right, axis=0), preferred_element_type=F32)
    pack(sums, out)


def add_kernel(added, got, order, out):
    parts = []
    for i in range(4):
        total = 0.0
        for j in range(4):
            total += got[j * 4 + i if added == 0 else i * 4 + j].astype(F32)
        parts.append(unfold(total))
    total = jnp.concatenate(parts, axis=1).astype(BF16)
    total = jnp.dot(order[...], total, preferred_element_type=F32).astype(BF16)
    for i in range(2):
        out[:, i, :] = total[i * 16 : (i + 1) * 16]


def call(kernel, name, n_in, *shapes, scalars=0):
    out = [jax.ShapeDtypeStruct(s, BF16) for s in shapes]
    spaces = [pltpu.SMEM] * scalars + [pltpu.VMEM] * (n_in - scalars)
    return pl.pallas_call(
        kernel,
        in_specs=[pl.BlockSpec(memory_space=space) for space in spaces],
        out_shape=out if len(out) > 1 else out[0],
        name=name,
        compiler_params=pltpu.CompilerParams(vmem_limit_bytes=32 * 1024 * 1024),
    )


def call_first(*operands):
    return pl.pallas_call(
        first_kernel,
        in_specs=[pl.BlockSpec(memory_space=pltpu.HBM)] * len(operands),
        out_shape=[
            jax.ShapeDtypeStruct((PAIRS, 2, 2 * TILE), BF16),
            jax.ShapeDtypeStruct((4, WIDTH), F32),
        ],
        scratch_shapes=[
            pltpu.VMEM((TILE, WIDTH), BF16),
            pltpu.VMEM((ROWS, COLS), jnp.int32),
            pltpu.VMEM((WIDTH, 4 * WIDTH), BF16),
            pltpu.SemaphoreType.DMA((7,)),
        ],
        name="project_first",
        compiler_params=pltpu.CompilerParams(vmem_limit_bytes=60 * 1024 * 1024),
    )(*operands)


def per_device(
    pair_input,
    pair_mask,
    out_norm_gain,
    out_w_in,
    out_final_gain,
    out_w_out,
    in_norm_gain,
    in_w_in,
    in_final_gain,
    in_w_out,
):
    out_norm_gain, out_final_gain, in_norm_gain, in_final_gain = (
        g.reshape(1, WIDTH) for g in (out_norm_gain, out_final_gain, in_norm_gain, in_final_gain)
    )
    left_order = one_hot(reorder((2, 4, 4, 4), (3, 1, 0, 2)))
    right_order = one_hot(reorder((2, 4, 4, 4), (3, 2, 1, 0)))
    out_rows = one_hot(reorder((ROWS, 32), (1, 0)))
    piece_order = one_hot(reorder((4, 2, 4), (1, 2, 0)))
    in_order = one_hot(reorder((2, 4, 4, 4), (1, 3, 0, 2)))
    place = np.full((2, ROWS, 4, 2, 4), -1)
    for i in range(2):
        place[i, :, :, i, :] = reorder((4, 4, ROWS), (2, 1, 0))
    in_rows = np.stack([one_hot(place[i], 16 * ROWS) for i in range(2)])
    left_order, right_order, out_rows, piece_order, in_order, in_rows = (
        jnp.asarray(t) for t in (left_order, right_order, out_rows, piece_order, in_order, in_rows)
    )
    core = lax.axis_index("core").reshape(1).astype(jnp.int32)

    def spread(sent, order):
        got = lax.all_to_all(sent, order, 0, 0, tiled=True)
        return got, lax.all_gather(got, "core", tiled=True)

    def collect(pieces, added):
        got = lax.all_to_all(pieces, PLANE, 0, 0, tiled=True)
        add = functools.partial(add_kernel, added)
        sums = call(add, "add_parts", 2, (16, 2, 4 * TILE))(got, piece_order)
        return lax.all_to_all(sums, LINE, 0, 0, tiled=True)

    pair = pair_input.reshape(TILE, WIDTH)
    sent, gains = call_first(
        pair,
        pair_mask,
        out_norm_gain,
        out_final_gain,
        in_norm_gain,
        in_final_gain,
        out_w_in,
    )
    own, both = spread(sent, OUT_CHANNEL)
    pieces = call(outgoing_kernel, "outgoing", 6, (16, 72, 128), scalars=1)(core, own, both, left_order, right_order, out_rows)
    tri = collect(pieces, 0)

    middle, sent = call(middle_kernel, "middle", 7, (TILE, WIDTH), (PAIRS, 2, 2 * TILE))(
        pair, pair_mask, tri, gains, out_w_in, out_w_out, in_w_in
    )
    _, both = spread(sent, IN_CHANNEL)
    pieces = call(incoming_kernel, "incoming", 4, (16, 72, 128), scalars=1)(
        core, both, in_order, in_rows
    )
    tri = collect(pieces, 1)
    out = call(last_kernel, "last", 5, (TILE, WIDTH))(middle, tri, gains, in_w_in, in_w_out)
    return out.reshape(ROWS, COLS, WIDTH)


def solution(mesh):
    fine = Mesh(
        mesh.devices.reshape([SIZES[a] for a in ROW + COL]), ROW + COL
    )
    placed = (P(ROW, COL, None), P(ROW, COL), P(), P(), P(), P(), P(), P(), P(), P())
    return jax.shard_map(
        per_device, mesh=fine, in_specs=placed, out_specs=P(ROW, COL, None), check_vma=False
    )
```

```python
import functools

import jax
import jax.numpy as jnp
import ml_dtypes
import numpy as np
from jax import lax
from jax.experimental import pallas as pl
from jax.experimental.pallas import tpu as pltpu
from jax.sharding import Mesh
from jax.sharding import PartitionSpec as P

ROW = ("zl", "y", "core")
COL = ("x", "zh")
SIZES = {"zl": 4, "y": 4, "core": 2, "x": 4, "zh": 4}
OUT_CHANNEL = ("y", "zh", "zl")
IN_CHANNEL = ("x", "zh", "zl")
LINE = ("zh", "zl")
PLANE = ("x", "y")

ROWS, COLS, WIDTH = 12, 24, 128
TILE = ROWS * COLS
PAIRS = WIDTH // 2
N = 384
F32, BF16 = jnp.float32, jnp.bfloat16


def one_hot(places, width=None):
    places = np.asarray(places).reshape(-1)
    table = np.zeros((len(places), width or len(places)), np.float32)
    table[np.arange(len(places))[places >= 0], places[places >= 0]] = 1
    return table.astype(ml_dtypes.bfloat16)


def reorder(sizes, order):
    return np.arange(np.prod(sizes)).reshape(sizes).transpose(order)


def layer_norm(values, gain):
    center = values - jnp.mean(values, axis=-1, keepdims=True)
    spread = jnp.mean(center * center, axis=-1, keepdims=True)
    return center * lax.rsqrt(spread + 1e-05) * gain


def flat_mask(mask):
    return jnp.concatenate([mask[i : i + 1] for i in range(ROWS)], axis=1)


def project(normed, mask, w_in):
    proj = lax.dot_general(
        w_in[:, : 4 * WIDTH], normed, (((0,), (1,)), ((), ())), preferred_element_type=F32
    )
    left = proj[:WIDTH] * jax.nn.sigmoid(proj[2 * WIDTH : 3 * WIDTH]) * mask
    right = proj[WIDTH : 2 * WIDTH] * jax.nn.sigmoid(proj[3 * WIDTH : 4 * WIDTH]) * mask
    return [jnp.concatenate([v[:PAIRS], v[PAIRS:]], axis=1).astype(BF16) for v in (left, right)]


def update(pair, tri, norm_gain, w_in, final_gain, w_out):
    final = layer_norm(tri.T, final_gain).astype(BF16)
    normed = layer_norm(pair, norm_gain).astype(BF16)
    gate = jax.nn.sigmoid(jnp.dot(normed, w_in[:, 4 * WIDTH :], preferred_element_type=F32))
    return (pair + jnp.dot(final, w_out, preferred_element_type=F32) * gate).astype(BF16)


def sums_of(tri):
    pair = [tri[:, i, :].astype(F32) for i in range(2)]
    return jnp.concatenate([v[:, i * TILE : (i + 1) * TILE] for v in pair for i in range(4)], axis=0)


def first_kernel(pair_ref, mask_ref, g0, g1, g2, g3, w_in, sent, gains, pair, mask, weights, sems):
    copies = [
        pltpu.make_async_copy(pair_ref, pair, sems.at[0]),
        pltpu.make_async_copy(mask_ref, mask, sems.at[1]),
        pltpu.make_async_copy(w_in.at[:, pl.ds(0, 4 * WIDTH)], weights, sems.at[2]),
    ]
    for i, gain in enumerate((g0, g1, g2, g3)):
        copies.append(pltpu.make_async_copy(gain, gains.at[pl.ds(i, 1)], sems.at[3 + i]))
    for copy in copies:
        copy.start()
    for copy in copies:
        copy.wait()
    normed = layer_norm(pair[...].astype(F32), gains[0:1]).astype(BF16)
    sent[:, 0, :], sent[:, 1, :] = project(normed, flat_mask(mask[...].astype(F32)), weights[...])


def middle_kernel(pair_ref, mask, tri, gains, w_in, w_out, next_w_in, middle, sent):
    pair = pair_ref[...].astype(F32)
    new = update(pair, sums_of(tri), gains[0:1], w_in, gains[1:2], w_out[...])
    middle[...] = new
    normed = layer_norm(new.astype(F32), gains[2:3]).astype(BF16)
    sent[:, 0, :], sent[:, 1, :] = project(normed, flat_mask(mask[...].astype(F32)), next_w_in)


def last_kernel(pair_ref, tri, gains, w_in, w_out, out):
    pair = pair_ref[...].astype(F32)
    out[...] = update(pair, sums_of(tri), gains[2:3], w_in, gains[3:4], w_out[...])


def chunks(side, wide):
    return jnp.concatenate(
        [
            jnp.concatenate([side[x * 32 : (x + 1) * 32, i * wide : (i + 1) * wide] for x in range(4)], axis=1)
            for i in range(ROWS)
        ],
        axis=0,
    )


def fold(strip):
    n = strip.shape[0] // 4
    rest = jnp.concatenate([strip[g * n : (g + 1) * n, 256:] for g in range(4)], axis=1)
    return jnp.concatenate([strip[:, :128], strip[:, 128:256], rest], axis=0)


def unfold(folded):
    n = folded.shape[0] // 9
    rest = jnp.concatenate([folded[8 * n :, g * 32 : (g + 1) * 32] for g in range(4)], axis=0)
    return jnp.concatenate([folded[: 4 * n], folded[4 * n : 8 * n], rest], axis=1)


def pack(sums, out):
    for x in range(4):
        strips = []
        for zh in range(4):
            at = (x * 4 + zh) * COLS
            strips.append(
                jnp.concatenate([sums[i * 32 : (i + 1) * 32, at : at + COLS] for i in range(ROWS)], axis=1)
            )
        for y in range(4):
            piece = jnp.concatenate([s[y * 8 : (y + 1) * 8] for s in strips], axis=0)
            out[x * 4 + y] = fold(piece).astype(BF16)


def outgoing_kernel(core, own, both, left_order, right_order, rows, out):
    left = own[:, 0, :].astype(F32)
    left = jnp.concatenate([left[:, :TILE], left[:, TILE:]], axis=0).astype(BF16)
    left = chunks(jnp.dot(left_order[...], left, preferred_element_type=F32), COLS)
    first = lax.broadcasted_iota(jnp.int32, left.shape, 0) % 8 < 4
    left = jnp.concatenate([jnp.where(first, left, 0.0), jnp.where(first, 0.0, left)], axis=1).astype(BF16)
    right = jnp.dot(right_order[...], both[:, 1, :], preferred_element_type=F32)
    right = jnp.concatenate([chunks(right[:, :TILE], COLS), chunks(right[:, TILE:], COLS)], axis=1)
    right = jnp.dot(rows[...], right.astype(BF16), preferred_element_type=F32).astype(BF16)
    sums = lax.dot_general(left, right, (((1,), (1,)), ((), ())), preferred_element_type=F32)
    pack(sums, out)


def incoming_kernel(core, both, order, rows, out):
    def operand(side, wide):
        return jnp.concatenate(
            [
                jnp.concatenate(
                    [side[g * 8 : (g + 1) * 8, k * COLS : k * COLS + wide] for g in range(16)], axis=1
                )
                for k in range(ROWS)
            ],
            axis=0,
        ).astype(BF16)

    left = jnp.dot(order[...], both[:, 0, :], preferred_element_type=F32)
    left = jnp.where(core[0] == 0, left, jnp.concatenate([left[:, ROWS:], left[:, :ROWS]], axis=1))
    left = [operand(left[:, i * TILE : (i + 1) * TILE], COLS // 2) for i in range(2)]
    left = [
        lax.dot_general(rows[i], left[i], (((1,), (1,)), ((), ())), preferred_element_type=F32)
        for i in range(2)
    ]
    left = jnp.concatenate(left, axis=1).astype(BF16)
    right = jnp.dot(order[...], both[:, 1, :], preferred_element_type=F32)
    right = [operand(right[:, i * TILE : (i + 1) * TILE], COLS) for i in range(2)]
    sums = jnp.dot(left, jnp.concatenate(right, axis=0), preferred_element_type=F32)
    pack(sums, out)


def add_kernel(added, got, order, out):
    parts = []
    for i in range(4):
        total = 0.0
        for j in range(4):
            total += got[j * 4 + i if added == 0 else i * 4 + j].astype(F32)
        parts.append(unfold(total))
    total = jnp.concatenate(parts, axis=1).astype(BF16)
    total = jnp.dot(order[...], total, preferred_element_type=F32).astype(BF16)
    for i in range(2):
        out[:, i, :] = total[i * 16 : (i + 1) * 16]


def call(kernel, name, n_in, *shapes, scalars=0):
    out = [jax.ShapeDtypeStruct(s, BF16) for s in shapes]
    spaces = [pltpu.SMEM] * scalars + [pltpu.VMEM] * (n_in - scalars)
    return pl.pallas_call(
        kernel,
        in_specs=[pl.BlockSpec(memory_space=space) for space in spaces],
        out_shape=out if len(out) > 1 else out[0],
        name=name,
        compiler_params=pltpu.CompilerParams(vmem_limit_bytes=32 * 1024 * 1024),
    )


def call_first(*operands):
    return pl.pallas_call(
        first_kernel,
        in_specs=[pl.BlockSpec(memory_space=pltpu.HBM)] * len(operands),
        out_shape=[
            jax.ShapeDtypeStruct((PAIRS, 2, 2 * TILE), BF16),
            jax.ShapeDtypeStruct((4, WIDTH), F32),
        ],
        scratch_shapes=[
            pltpu.VMEM((TILE, WIDTH), BF16),
            pltpu.VMEM((ROWS, COLS), jnp.int32),
            pltpu.VMEM((WIDTH, 4 * WIDTH), BF16),
            pltpu.SemaphoreType.DMA((7,)),
        ],
        name="project_first",
        compiler_params=pltpu.CompilerParams(vmem_limit_bytes=60 * 1024 * 1024),
    )(*operands)


def per_device(
    pair_input,
    pair_mask,
    out_norm_gain,
    out_w_in,
    out_final_gain,
    out_w_out,
    in_norm_gain,
    in_w_in,
    in_final_gain,
    in_w_out,
):
    out_norm_gain, out_final_gain, in_norm_gain, in_final_gain = (
        g.reshape(1, WIDTH) for g in (out_norm_gain, out_final_gain, in_norm_gain, in_final_gain)
    )
    left_order = one_hot(reorder((2, 4, 4, 4), (2, 1, 0, 3)))
    right_order = one_hot(reorder((2, 4, 4, 4), (2, 3, 1, 0)))
    out_rows = one_hot(reorder((ROWS, 32), (1, 0)))
    piece_order = one_hot(reorder((4, 2, 4), (1, 0, 2)))
    in_order = one_hot(reorder((2, 4, 4, 4), (1, 2, 0, 3)))
    place = np.full((2, ROWS, 4, 2, 4), -1)
    for i in range(2):
        place[i, :, :, i, :] = reorder((4, 4, ROWS), (2, 1, 0))
    in_rows = np.stack([one_hot(place[i], 16 * ROWS) for i in range(2)])
    left_order, right_order, out_rows, piece_order, in_order, in_rows = (
        jnp.asarray(t) for t in (left_order, right_order, out_rows, piece_order, in_order, in_rows)
    )
    core = lax.axis_index("core").reshape(1).astype(jnp.int32)

    def spread(sent, order):
        got = lax.all_to_all(sent, order, 0, 0, tiled=True)
        return got, lax.all_gather(got, "core", tiled=True)

    def collect(pieces, added):
        got = lax.all_to_all(pieces, PLANE, 0, 0, tiled=True)
        add = functools.partial(add_kernel, added)
        sums = call(add, "add_parts", 2, (16, 2, 4 * TILE))(got, piece_order)
        return lax.all_to_all(sums, LINE, 0, 0, tiled=True)

    pair = pair_input.reshape(TILE, WIDTH)
    sent, gains = call_first(
        pair,
        pair_mask,
        out_norm_gain,
        out_final_gain,
        in_norm_gain,
        in_final_gain,
        out_w_in,
    )
    own, both = spread(sent, OUT_CHANNEL)
    pieces = call(outgoing_kernel, "outgoing", 6, (16, 72, 128), scalars=1)(core, own, both, left_order, right_order, out_rows)
    tri = collect(pieces, 0)

    middle, sent = call(middle_kernel, "middle", 7, (TILE, WIDTH), (PAIRS, 2, 2 * TILE))(
        pair, pair_mask, tri, gains, out_w_in, out_w_out, in_w_in
    )
    _, both = spread(sent, IN_CHANNEL)
    pieces = call(incoming_kernel, "incoming", 4, (16, 72, 128), scalars=1)(
        core, both, in_order, in_rows
    )
    tri = collect(pieces, 1)
    out = call(last_kernel, "last", 5, (TILE, WIDTH))(middle, tri, gains, in_w_in, in_w_out)
    return out.reshape(ROWS, COLS, WIDTH)


def solution(mesh):
    fine = Mesh(
        mesh.devices.reshape([SIZES[a] for a in ROW + COL]), ROW + COL
    )
    placed = (P(ROW, COL, None), P(ROW, COL), P(), P(), P(), P(), P(), P(), P(), P())
    return jax.shard_map(
        per_device, mesh=fine, in_specs=placed, out_specs=P(ROW, COL, None), check_vma=False
    )
```

```python
import functools

import jax
import jax.numpy as jnp
import ml_dtypes
import numpy as np
from jax import lax
from jax.experimental import pallas as pl
from jax.experimental.pallas import tpu as pltpu
from jax.sharding import Mesh
from jax.sharding import PartitionSpec as P

ROW = ("zl", "y", "core")
COL = ("x", "zh")
SIZES = {"zl": 4, "y": 4, "core": 2, "x": 4, "zh": 4}
OUT_CHANNEL = ("y", "zh", "zl")
IN_CHANNEL = ("x", "zh", "zl")
LINE = ("zh", "zl")
PLANE = ("x", "y")

ROWS, COLS, WIDTH = 12, 24, 128
TILE = ROWS * COLS
PAIRS = WIDTH // 2
N = 384
F32, BF16 = jnp.float32, jnp.bfloat16


def one_hot(places, width=None):
    places = np.asarray(places).reshape(-1)
    table = np.zeros((len(places), width or len(places)), np.float32)
    table[np.arange(len(places))[places >= 0], places[places >= 0]] = 1
    return table.astype(ml_dtypes.bfloat16)


def reorder(sizes, order):
    return np.arange(np.prod(sizes)).reshape(sizes).transpose(order)


def layer_norm(values, gain):
    center = values - jnp.mean(values, axis=-1, keepdims=True)
    spread = jnp.mean(center * center, axis=-1, keepdims=True)
    return center * lax.rsqrt(spread + 1e-05) * gain


def flat_mask(mask):
    return jnp.concatenate([mask[i : i + 1] for i in range(ROWS)], axis=1)


def project(normed, mask, w_in):
    proj = lax.dot_general(
        w_in[:, : 4 * WIDTH], normed, (((0,), (1,)), ((), ())), preferred_element_type=F32
    )
    left = proj[:WIDTH] * jax.nn.sigmoid(proj[2 * WIDTH : 3 * WIDTH]) * mask
    right = proj[WIDTH : 2 * WIDTH] * jax.nn.sigmoid(proj[3 * WIDTH : 4 * WIDTH]) * mask
    return [jnp.concatenate([v[:PAIRS], v[PAIRS:]], axis=1).astype(BF16) for v in (left, right)]


def update(pair, tri, norm_gain, w_in, final_gain, w_out):
    final = layer_norm(tri.T, final_gain).astype(BF16)
    normed = layer_norm(pair, norm_gain).astype(BF16)
    gate = jax.nn.sigmoid(jnp.dot(normed, w_in[:, 4 * WIDTH :], preferred_element_type=F32))
    return (pair + jnp.dot(final, w_out, preferred_element_type=F32) * gate).astype(BF16)


def sums_of(tri):
    pair = [tri[:, i, :].astype(F32) for i in range(2)]
    return jnp.concatenate([v[:, i * TILE : (i + 1) * TILE] for v in pair for i in range(4)], axis=0)


def first_kernel(pair_ref, mask_ref, g0, g1, g2, g3, w_in, sent, gains, pair, mask, weights, sems):
    copies = [
        pltpu.make_async_copy(pair_ref, pair, sems.at[0]),
        pltpu.make_async_copy(mask_ref, mask, sems.at[1]),
        pltpu.make_async_copy(w_in.at[:, pl.ds(0, 4 * WIDTH)], weights, sems.at[2]),
    ]
    for i, gain in enumerate((g0, g1, g2, g3)):
        copies.append(pltpu.make_async_copy(gain, gains.at[pl.ds(i, 1)], sems.at[3 + i]))
    for copy in copies:
        copy.start()
    for copy in copies:
        copy.wait()
    normed = layer_norm(pair[...].astype(F32), gains[0:1]).astype(BF16)
    sent[:, 0, :], sent[:, 1, :] = project(normed, flat_mask(mask[...].astype(F32)), weights[...])


def middle_kernel(pair_ref, mask, tri, gains, w_in, w_out, next_w_in, middle, sent):
    pair = pair_ref[...].astype(F32)
    new = update(pair, sums_of(tri), gains[0:1], w_in, gains[1:2], w_out[...])
    middle[...] = new
    normed = layer_norm(new.astype(F32), gains[2:3]).astype(BF16)
    sent[:, 0, :], sent[:, 1, :] = project(normed, flat_mask(mask[...].astype(F32)), next_w_in)


def last_kernel(pair_ref, tri, gains, w_in, w_out, out):
    pair = pair_ref[...].astype(F32)
    out[...] = update(pair, sums_of(tri), gains[2:3], w_in, gains[3:4], w_out[...])


def chunks(side, wide):
    return jnp.concatenate(
        [
            jnp.concatenate([side[x * 32 : (x + 1) * 32, i * wide : (i + 1) * wide] for x in range(4)], axis=1)
            for i in range(ROWS)
        ],
        axis=0,
    )


def fold(strip):
    n = strip.shape[0] // 4
    rest = jnp.concatenate([strip[g * n : (g + 1) * n, 256:] for g in range(4)], axis=1)
    return jnp.concatenate([strip[:, :128], strip[:, 128:256], rest], axis=0)


def unfold(folded):
    n = folded.shape[0] // 9
    rest = jnp.concatenate([folded[8 * n :, g * 32 : (g + 1) * 32] for g in range(4)], axis=0)
    return jnp.concatenate([folded[: 4 * n], folded[4 * n : 8 * n], rest], axis=1)


def pack(sums, out):
    for x in range(4):
        strips = []
        for zh in range(4):
            at = (x * 4 + zh) * COLS
            strips.append(
                jnp.concatenate([sums[i * 32 : (i + 1) * 32, at : at + COLS] for i in range(ROWS)], axis=1)
            )
        for y in range(4):
            piece = jnp.concatenate([s[y * 8 : (y + 1) * 8] for s in strips], axis=0)
            out[x * 4 + y] = fold(piece).astype(BF16)


def outgoing_kernel(core, own, both, left_order, right_order, rows, out):
    left = own[:, 0, :].astype(F32)
    left = jnp.concatenate([left[:, :TILE], left[:, TILE:]], axis=0).astype(BF16)
    left = chunks(jnp.dot(left_order[...], left, preferred_element_type=F32), COLS)
    first = lax.broadcasted_iota(jnp.int32, left.shape, 0) % 8 < 4
    left = jnp.concatenate([jnp.where(first, left, 0.0), jnp.where(first, 0.0, left)], axis=1).astype(BF16)
    right = jnp.dot(right_order[...], both[:, 1, :], preferred_element_type=F32)
    right = jnp.concatenate([chunks(right[:, :TILE], COLS), chunks(right[:, TILE:], COLS)], axis=1)
    blocks = []
    for zl in range(4):
        block = [right[i * 32 + zl * 8 : i * 32 + (zl + 1) * 8] for i in range(ROWS)]
        block = jnp.concatenate(block, axis=0).astype(BF16)
        blocks.append(jnp.dot(rows[...], block, preferred_element_type=F32))
    right = jnp.concatenate(blocks, axis=0).astype(BF16)
    sums = lax.dot_general(left, right, (((1,), (1,)), ((), ())), preferred_element_type=F32)
    pack(sums, out)


def by_column(side):
    return jnp.concatenate(
        [side[c * PAIRS + g * 4 : c * PAIRS + (g + 1) * 4] for g in range(16) for c in range(2)], axis=0
    )


def incoming_kernel(core, both, rows, out):
    def operand(side, wide):
        return jnp.concatenate(
            [
                jnp.concatenate(
                    [side[g * 8 : (g + 1) * 8, k * COLS : k * COLS + wide] for g in range(16)], axis=1
                )
                for k in range(ROWS)
            ],
            axis=0,
        ).astype(BF16)

    left = by_column(both[:, 0, :].astype(F32))
    left = jnp.where(core[0] == 0, left, jnp.concatenate([left[:, ROWS:], left[:, :ROWS]], axis=1))
    left = [operand(left[:, i * TILE : (i + 1) * TILE], COLS // 2) for i in range(2)]
    left = [
        lax.dot_general(rows[i], left[i], (((1,), (1,)), ((), ())), preferred_element_type=F32)
        for i in range(2)
    ]
    left = jnp.concatenate(left, axis=1).astype(BF16)
    right = by_column(both[:, 1, :].astype(F32))
    right = [operand(right[:, i * TILE : (i + 1) * TILE], COLS) for i in range(2)]
    sums = jnp.dot(left, jnp.concatenate(right, axis=0), preferred_element_type=F32)
    pack(sums, out)


def add_kernel(added, got, order, out):
    parts = []
    for i in range(4):
        total = 0.0
        for j in range(4):
            total += got[j * 4 + i if added == 0 else i * 4 + j].astype(F32)
        parts.append(unfold(total))
    total = jnp.concatenate(parts, axis=1).astype(BF16)
    total = jnp.dot(order[...], total, preferred_element_type=F32).astype(BF16)
    for i in range(2):
        out[:, i, :] = total[i * 16 : (i + 1) * 16]


def call(kernel, name, n_in, *shapes, scalars=0):
    out = [jax.ShapeDtypeStruct(s, BF16) for s in shapes]
    spaces = [pltpu.SMEM] * scalars + [pltpu.VMEM] * (n_in - scalars)
    return pl.pallas_call(
        kernel,
        in_specs=[pl.BlockSpec(memory_space=space) for space in spaces],
        out_shape=out if len(out) > 1 else out[0],
        name=name,
        compiler_params=pltpu.CompilerParams(vmem_limit_bytes=32 * 1024 * 1024),
    )


def call_first(*operands):
    return pl.pallas_call(
        first_kernel,
        in_specs=[pl.BlockSpec(memory_space=pltpu.HBM)] * len(operands),
        out_shape=[
            jax.ShapeDtypeStruct((PAIRS, 2, 2 * TILE), BF16),
            jax.ShapeDtypeStruct((4, WIDTH), F32),
        ],
        scratch_shapes=[
            pltpu.VMEM((TILE, WIDTH), BF16),
            pltpu.VMEM((ROWS, COLS), jnp.int32),
            pltpu.VMEM((WIDTH, 4 * WIDTH), BF16),
            pltpu.SemaphoreType.DMA((7,)),
        ],
        name="project_first",
        compiler_params=pltpu.CompilerParams(vmem_limit_bytes=60 * 1024 * 1024),
    )(*operands)


def per_device(
    pair_input,
    pair_mask,
    out_norm_gain,
    out_w_in,
    out_final_gain,
    out_w_out,
    in_norm_gain,
    in_w_in,
    in_final_gain,
    in_w_out,
):
    out_norm_gain, out_final_gain, in_norm_gain, in_final_gain = (
        g.reshape(1, WIDTH) for g in (out_norm_gain, out_final_gain, in_norm_gain, in_final_gain)
    )
    left_order = one_hot(reorder((2, 4, 4, 4), (2, 1, 0, 3)))
    right_order = one_hot(reorder((2, 4, 4, 4), (2, 3, 1, 0)))
    out_rows = one_hot(reorder((ROWS, 8), (1, 0)))
    piece_order = one_hot(reorder((4, 2, 4), (1, 0, 2)))
    place = np.full((2, ROWS, 4, 2, 4), -1)
    for i in range(2):
        place[i, :, :, i, :] = reorder((4, 4, ROWS), (2, 1, 0))
    in_rows = np.stack([one_hot(place[i], 16 * ROWS) for i in range(2)])
    left_order, right_order, out_rows, piece_order, in_rows = (
        jnp.asarray(t) for t in (left_order, right_order, out_rows, piece_order, in_rows)
    )
    core = lax.axis_index("core").reshape(1).astype(jnp.int32)

    def spread(sent, order):
        got = lax.all_to_all(sent, order, 0, 0, tiled=True)
        return got, lax.all_gather(got, "core", tiled=True)

    def collect(pieces, added):
        got = lax.all_to_all(pieces, PLANE, 0, 0, tiled=True)
        add = functools.partial(add_kernel, added)
        sums = call(add, "add_parts", 2, (16, 2, 4 * TILE))(got, piece_order)
        return lax.all_to_all(sums, LINE, 0, 0, tiled=True)

    pair = pair_input.reshape(TILE, WIDTH)
    sent, gains = call_first(
        pair,
        pair_mask,
        out_norm_gain,
        out_final_gain,
        in_norm_gain,
        in_final_gain,
        out_w_in,
    )
    own, both = spread(sent, OUT_CHANNEL)
    pieces = call(outgoing_kernel, "outgoing", 6, (16, 72, 128), scalars=1)(core, own, both, left_order, right_order, out_rows)
    tri = collect(pieces, 0)

    middle, sent = call(middle_kernel, "middle", 7, (TILE, WIDTH), (PAIRS, 2, 2 * TILE))(
        pair, pair_mask, tri, gains, out_w_in, out_w_out, in_w_in
    )
    _, both = spread(sent, IN_CHANNEL)
    pieces = call(incoming_kernel, "incoming", 3, (16, 72, 128), scalars=1)(
        core, both, in_rows
    )
    tri = collect(pieces, 1)
    out = call(last_kernel, "last", 5, (TILE, WIDTH))(middle, tri, gains, in_w_in, in_w_out)
    return out.reshape(ROWS, COLS, WIDTH)


def solution(mesh):
    fine = Mesh(
        mesh.devices.reshape([SIZES[a] for a in ROW + COL]), ROW + COL
    )
    placed = (P(ROW, COL, None), P(ROW, COL), P(), P(), P(), P(), P(), P(), P(), P())
    return jax.shard_map(
        per_device, mesh=fine, in_specs=placed, out_specs=P(ROW, COL, None), check_vma=False
    )
```

```python
import functools

import jax
import jax.numpy as jnp
import ml_dtypes
import numpy as np
from jax import lax
from jax.experimental import pallas as pl
from jax.experimental.pallas import tpu as pltpu
from jax.sharding import Mesh
from jax.sharding import PartitionSpec as P

ROW = ("zl", "y", "core")
COL = ("x", "zh")
SIZES = {"zl": 4, "y": 4, "core": 2, "x": 4, "zh": 4}
OUT_CHANNEL = ("y", "zh", "zl")
IN_CHANNEL = ("x", "zh", "zl")
LINE = ("zh", "zl")
PLANE = ("x", "y")

ROWS, COLS, WIDTH = 12, 24, 128
TILE = ROWS * COLS
PAIRS = WIDTH // 2
N = 384
F32, BF16 = jnp.float32, jnp.bfloat16


def one_hot(places, width=None):
    places = np.asarray(places).reshape(-1)
    table = np.zeros((len(places), width or len(places)), np.float32)
    table[np.arange(len(places))[places >= 0], places[places >= 0]] = 1
    return table.astype(ml_dtypes.bfloat16)


def reorder(sizes, order):
    return np.arange(np.prod(sizes)).reshape(sizes).transpose(order)


def layer_norm(values, gain):
    center = values - jnp.mean(values, axis=-1, keepdims=True)
    spread = jnp.mean(center * center, axis=-1, keepdims=True)
    return center * lax.rsqrt(spread + 1e-05) * gain


def flat_mask(mask):
    return jnp.concatenate([mask[i : i + 1] for i in range(ROWS)], axis=1)


def project(normed, mask, w_in):
    proj = lax.dot_general(
        w_in[:, : 4 * WIDTH], normed, (((0,), (1,)), ((), ())), preferred_element_type=F32
    )
    left = proj[:WIDTH] * jax.nn.sigmoid(proj[2 * WIDTH : 3 * WIDTH]) * mask
    right = proj[WIDTH : 2 * WIDTH] * jax.nn.sigmoid(proj[3 * WIDTH : 4 * WIDTH]) * mask
    return [jnp.concatenate([v[:PAIRS], v[PAIRS:]], axis=1).astype(BF16) for v in (left, right)]


def update(pair, tri, norm_gain, w_in, final_gain, w_out):
    final = layer_norm(tri.T, final_gain).astype(BF16)
    normed = layer_norm(pair, norm_gain).astype(BF16)
    gate = jax.nn.sigmoid(jnp.dot(normed, w_in[:, 4 * WIDTH :], preferred_element_type=F32))
    return (pair + jnp.dot(final, w_out, preferred_element_type=F32) * gate).astype(BF16)


def sums_of(tri):
    pair = [tri[:, i, :].astype(F32) for i in range(2)]
    return jnp.concatenate([v[:, i * TILE : (i + 1) * TILE] for v in pair for i in range(4)], axis=0)


def first_kernel(pair_ref, mask_ref, g0, g1, g2, g3, w_in, sent, gains, pair, mask, weights, sems):
    copies = [
        pltpu.make_async_copy(pair_ref, pair, sems.at[0]),
        pltpu.make_async_copy(mask_ref, mask, sems.at[1]),
        pltpu.make_async_copy(w_in.at[:, pl.ds(0, 4 * WIDTH)], weights, sems.at[2]),
    ]
    for i, gain in enumerate((g0, g1, g2, g3)):
        copies.append(pltpu.make_async_copy(gain, gains.at[pl.ds(i, 1)], sems.at[3 + i]))
    for copy in copies:
        copy.start()
    for copy in copies:
        copy.wait()
    normed = layer_norm(pair[...].astype(F32), gains[0:1]).astype(BF16)
    sent[:, 0, :], sent[:, 1, :] = project(normed, flat_mask(mask[...].astype(F32)), weights[...])


def middle_kernel(pair_ref, mask, tri, gains, w_in, w_out, next_w_in, middle, sent):
    pair = pair_ref[...].astype(F32)
    new = update(pair, sums_of(tri), gains[0:1], w_in, gains[1:2], w_out[...])
    middle[...] = new
    normed = layer_norm(new.astype(F32), gains[2:3]).astype(BF16)
    sent[:, 0, :], sent[:, 1, :] = project(normed, flat_mask(mask[...].astype(F32)), next_w_in)


def last_kernel(pair_ref, tri, gains, w_in, w_out, out):
    pair = pair_ref[...].astype(F32)
    out[...] = update(pair, sums_of(tri), gains[2:3], w_in, gains[3:4], w_out[...])


def chunks(side, wide):
    return jnp.concatenate(
        [
            jnp.concatenate([side[x * 32 : (x + 1) * 32, i * wide : (i + 1) * wide] for x in range(4)], axis=1)
            for i in range(ROWS)
        ],
        axis=0,
    )


def fold(strip):
    n = strip.shape[0] // 4
    rest = jnp.concatenate([strip[g * n : (g + 1) * n, 256:] for g in range(4)], axis=1)
    return jnp.concatenate([strip[:, :128], strip[:, 128:256], rest], axis=0)


def unfold(folded):
    n = folded.shape[0] // 9
    rest = jnp.concatenate([folded[8 * n :, g * 32 : (g + 1) * 32] for g in range(4)], axis=0)
    return jnp.concatenate([folded[: 4 * n], folded[4 * n : 8 * n], rest], axis=1)


def pack(sums, out):
    for x in range(4):
        strips = []
        for zh in range(4):
            at = (x * 4 + zh) * COLS
            strips.append(
                jnp.concatenate([sums[i * 32 : (i + 1) * 32, at : at + COLS] for i in range(ROWS)], axis=1)
            )
        for y in range(4):
            piece = jnp.concatenate([s[y * 8 : (y + 1) * 8] for s in strips], axis=0)
            out[x * 4 + y] = fold(piece).astype(BF16)


def by_zh(side):
    starts = [c * PAIRS + y * 16 + zh * 4 for zh in range(4) for y in range(4) for c in range(2)]
    return jnp.concatenate([side[i : i + 4] for i in starts], axis=0)


def outgoing_kernel(core, own, both, rows, out):
    left = own[:, 0, :].astype(F32)
    left = by_zh(jnp.concatenate([left[:, :TILE], left[:, TILE:]], axis=0))
    left = chunks(left, COLS)
    first = lax.broadcasted_iota(jnp.int32, left.shape, 0) % 8 < 4
    left = jnp.concatenate([jnp.where(first, left, 0.0), jnp.where(first, 0.0, left)], axis=1).astype(BF16)
    right = by_zh(both[:, 1, :].astype(F32))
    right = jnp.concatenate([chunks(right[:, :TILE], COLS), chunks(right[:, TILE:], COLS)], axis=1)
    right = jnp.dot(rows[...], right.astype(BF16), preferred_element_type=F32).astype(BF16)
    sums = lax.dot_general(left, right, (((1,), (1,)), ((), ())), preferred_element_type=F32)
    pack(sums, out)


def by_column(side):
    return jnp.concatenate(
        [side[c * PAIRS + g * 4 : c * PAIRS + (g + 1) * 4] for g in range(16) for c in range(2)], axis=0
    )


def incoming_kernel(core, both, rows, out):
    def operand(side, wide):
        return jnp.concatenate(
            [
                jnp.concatenate(
                    [side[g * 8 : (g + 1) * 8, k * COLS : k * COLS + wide] for g in range(16)], axis=1
                )
                for k in range(ROWS)
            ],
            axis=0,
        ).astype(BF16)

    left = by_column(both[:, 0, :].astype(F32))
    left = jnp.where(core[0] == 0, left, jnp.concatenate([left[:, ROWS:], left[:, :ROWS]], axis=1))
    left = [operand(left[:, i * TILE : (i + 1) * TILE], COLS // 2) for i in range(2)]
    left = [
        lax.dot_general(rows[i], left[i], (((1,), (1,)), ((), ())), preferred_element_type=F32)
        for i in range(2)
    ]
    left = jnp.concatenate(left, axis=1).astype(BF16)
    right = by_column(both[:, 1, :].astype(F32))
    right = [operand(right[:, i * TILE : (i + 1) * TILE], COLS) for i in range(2)]
    sums = jnp.dot(left, jnp.concatenate(right, axis=0), preferred_element_type=F32)
    pack(sums, out)


def add_kernel(added, got, out):
    parts = []
    for i in range(4):
        total = 0.0
        for j in range(4):
            total += got[j * 4 + i if added == 0 else i * 4 + j].astype(F32)
        parts.append(unfold(total))
    total = jnp.concatenate(parts, axis=1)
    for i in range(2):
        rows = [total[zh * 8 + i * 4 : zh * 8 + i * 4 + 4] for zh in range(4)]
        out[:, i, :] = jnp.concatenate(rows, axis=0).astype(BF16)


def call(kernel, name, n_in, *shapes, scalars=0):
    out = [jax.ShapeDtypeStruct(s, BF16) for s in shapes]
    spaces = [pltpu.SMEM] * scalars + [pltpu.VMEM] * (n_in - scalars)
    return pl.pallas_call(
        kernel,
        in_specs=[pl.BlockSpec(memory_space=space) for space in spaces],
        out_shape=out if len(out) > 1 else out[0],
        name=name,
        compiler_params=pltpu.CompilerParams(vmem_limit_bytes=32 * 1024 * 1024),
    )


def call_first(*operands):
    return pl.pallas_call(
        first_kernel,
        in_specs=[pl.BlockSpec(memory_space=pltpu.HBM)] * len(operands),
        out_shape=[
            jax.ShapeDtypeStruct((PAIRS, 2, 2 * TILE), BF16),
            jax.ShapeDtypeStruct((4, WIDTH), F32),
        ],
        scratch_shapes=[
            pltpu.VMEM((TILE, WIDTH), BF16),
            pltpu.VMEM((ROWS, COLS), jnp.int32),
            pltpu.VMEM((WIDTH, 4 * WIDTH), BF16),
            pltpu.SemaphoreType.DMA((7,)),
        ],
        name="project_first",
        compiler_params=pltpu.CompilerParams(vmem_limit_bytes=60 * 1024 * 1024),
    )(*operands)


def per_device(
    pair_input,
    pair_mask,
    out_norm_gain,
    out_w_in,
    out_final_gain,
    out_w_out,
    in_norm_gain,
    in_w_in,
    in_final_gain,
    in_w_out,
):
    out_norm_gain, out_final_gain, in_norm_gain, in_final_gain = (
        g.reshape(1, WIDTH) for g in (out_norm_gain, out_final_gain, in_norm_gain, in_final_gain)
    )
    out_rows = one_hot(reorder((ROWS, 4, 2, 4), (3, 1, 2, 0)))
    place = np.full((2, ROWS, 4, 2, 4), -1)
    for i in range(2):
        place[i, :, :, i, :] = reorder((4, 4, ROWS), (2, 1, 0))
    in_rows = np.stack([one_hot(place[i], 16 * ROWS) for i in range(2)])
    out_rows, in_rows = (
        jnp.asarray(t) for t in (out_rows, in_rows)
    )
    core = lax.axis_index("core").reshape(1).astype(jnp.int32)

    def spread(sent, order):
        got = lax.all_to_all(sent, order, 0, 0, tiled=True)
        return got, lax.all_gather(got, "core", tiled=True)

    def collect(pieces, added):
        got = lax.all_to_all(pieces, PLANE, 0, 0, tiled=True)
        add = functools.partial(add_kernel, added)
        sums = call(add, "add_parts", 1, (16, 2, 4 * TILE))(got)
        return lax.all_to_all(sums, LINE, 0, 0, tiled=True)

    pair = pair_input.reshape(TILE, WIDTH)
    sent, gains = call_first(
        pair,
        pair_mask,
        out_norm_gain,
        out_final_gain,
        in_norm_gain,
        in_final_gain,
        out_w_in,
    )
    own, both = spread(sent, OUT_CHANNEL)
    pieces = call(outgoing_kernel, "outgoing", 4, (16, 72, 128), scalars=1)(core, own, both, out_rows)
    tri = collect(pieces, 0)

    middle, sent = call(middle_kernel, "middle", 7, (TILE, WIDTH), (PAIRS, 2, 2 * TILE))(
        pair, pair_mask, tri, gains, out_w_in, out_w_out, in_w_in
    )
    _, both = spread(sent, IN_CHANNEL)
    pieces = call(incoming_kernel, "incoming", 3, (16, 72, 128), scalars=1)(
        core, both, in_rows
    )
    tri = collect(pieces, 1)
    out = call(last_kernel, "last", 5, (TILE, WIDTH))(middle, tri, gains, in_w_in, in_w_out)
    return out.reshape(ROWS, COLS, WIDTH)


def solution(mesh):
    fine = Mesh(
        mesh.devices.reshape([SIZES[a] for a in ROW + COL]), ROW + COL
    )
    placed = (P(ROW, COL, None), P(ROW, COL), P(), P(), P(), P(), P(), P(), P(), P())
    return jax.shard_map(
        per_device, mesh=fine, in_specs=placed, out_specs=P(ROW, COL, None), check_vma=False
    )
```

```python
import functools

import jax
import jax.numpy as jnp
import ml_dtypes
import numpy as np
from jax import lax
from jax.experimental import pallas as pl
from jax.experimental.pallas import tpu as pltpu
from jax.sharding import Mesh
from jax.sharding import PartitionSpec as P

ROW = ("zl", "y", "core")
COL = ("x", "zh")
SIZES = {"zl": 4, "y": 4, "core": 2, "x": 4, "zh": 4}
OUT_CHANNEL = ("y", "zh", "zl")
IN_CHANNEL = ("x", "zh", "zl")
LINE = ("zh", "zl")
PLANE = ("x", "y")

ROWS, COLS, WIDTH = 12, 24, 128
TILE = ROWS * COLS
PAIRS = WIDTH // 2
N = 384
F32, BF16 = jnp.float32, jnp.bfloat16


def one_hot(places, width=None):
    places = np.asarray(places).reshape(-1)
    table = np.zeros((len(places), width or len(places)), np.float32)
    table[np.arange(len(places))[places >= 0], places[places >= 0]] = 1
    return table.astype(ml_dtypes.bfloat16)


def reorder(sizes, order):
    return np.arange(np.prod(sizes)).reshape(sizes).transpose(order)


def layer_norm(values, gain):
    center = values - jnp.mean(values, axis=-1, keepdims=True)
    spread = jnp.mean(center * center, axis=-1, keepdims=True)
    return center * lax.rsqrt(spread + 1e-05) * gain


def flat_mask(mask):
    return jnp.concatenate([mask[i : i + 1] for i in range(ROWS)], axis=1)


def project(normed, mask, w_in):
    proj = lax.dot_general(
        w_in[:, : 4 * WIDTH], normed, (((0,), (1,)), ((), ())), preferred_element_type=F32
    )
    left = proj[:WIDTH] * jax.nn.sigmoid(proj[2 * WIDTH : 3 * WIDTH]) * mask
    right = proj[WIDTH : 2 * WIDTH] * jax.nn.sigmoid(proj[3 * WIDTH : 4 * WIDTH]) * mask
    return [jnp.concatenate([v[:PAIRS], v[PAIRS:]], axis=1).astype(BF16) for v in (left, right)]


def update(pair, tri, norm_gain, w_in, final_gain, w_out):
    final = layer_norm(tri.T, final_gain).astype(BF16)
    normed = layer_norm(pair, norm_gain).astype(BF16)
    gate = jax.nn.sigmoid(jnp.dot(normed, w_in[:, 4 * WIDTH :], preferred_element_type=F32))
    return (pair + jnp.dot(final, w_out, preferred_element_type=F32) * gate).astype(BF16)


def sums_of(tri):
    pair = [tri[:, i, :].astype(F32) for i in range(2)]
    return jnp.concatenate([v[:, i * TILE : (i + 1) * TILE] for v in pair for i in range(4)], axis=0)


def first_kernel(pair_ref, mask_ref, g0, g1, g2, g3, w_in, sent, gains, pair, mask, weights, sems):
    copies = [
        pltpu.make_async_copy(pair_ref, pair, sems.at[0]),
        pltpu.make_async_copy(mask_ref, mask, sems.at[1]),
        pltpu.make_async_copy(w_in.at[:, pl.ds(0, 4 * WIDTH)], weights, sems.at[2]),
    ]
    for i, gain in enumerate((g0, g1, g2, g3)):
        copies.append(pltpu.make_async_copy(gain, gains.at[pl.ds(i, 1)], sems.at[3 + i]))
    for copy in copies:
        copy.start()
    for copy in copies:
        copy.wait()
    normed = layer_norm(pair[...].astype(F32), gains[0:1]).astype(BF16)
    sent[:, 0, :], sent[:, 1, :] = project(normed, flat_mask(mask[...].astype(F32)), weights[...])


def middle_kernel(pair_ref, mask, tri, gains, w_in, w_out, next_w_in, middle, sent):
    pair = pair_ref[...].astype(F32)
    new = update(pair, sums_of(tri), gains[0:1], w_in, gains[1:2], w_out[...])
    middle[...] = new
    normed = layer_norm(new.astype(F32), gains[2:3]).astype(BF16)
    sent[:, 0, :], sent[:, 1, :] = project(normed, flat_mask(mask[...].astype(F32)), next_w_in)


def last_kernel(pair_ref, tri, gains, w_in, w_out, out):
    pair = pair_ref[...].astype(F32)
    out[...] = update(pair, sums_of(tri), gains[2:3], w_in, gains[3:4], w_out[...])


def chunks(side, wide):
    return jnp.concatenate(
        [
            jnp.concatenate([side[x * 32 : (x + 1) * 32, i * wide : (i + 1) * wide] for x in range(4)], axis=1)
            for i in range(ROWS)
        ],
        axis=0,
    )


def fold(strip):
    n = strip.shape[0] // 4
    rest = jnp.concatenate([strip[g * n : (g + 1) * n, 256:] for g in range(4)], axis=1)
    return jnp.concatenate([strip[:, :128], strip[:, 128:256], rest], axis=0)


def unfold(folded):
    n = folded.shape[0] // 9
    rest = jnp.concatenate([folded[8 * n :, g * 32 : (g + 1) * 32] for g in range(4)], axis=0)
    return jnp.concatenate([folded[: 4 * n], folded[4 * n : 8 * n], rest], axis=1)


def pack(sums, out):
    for x in range(4):
        strips = []
        for zh in range(4):
            at = (x * 4 + zh) * COLS
            strips.append(
                jnp.concatenate([sums[i * 32 : (i + 1) * 32, at : at + COLS] for i in range(ROWS)], axis=1)
            )
        for y in range(4):
            piece = jnp.concatenate([s[y * 8 : (y + 1) * 8] for s in strips], axis=0)
            out[x * 4 + y] = fold(piece).astype(BF16)


def by_zh(side):
    starts = [c * PAIRS + y * 16 + zh * 4 for zh in range(4) for y in range(4) for c in range(2)]
    return jnp.concatenate([side[i : i + 4] for i in starts], axis=0)


def outgoing_kernel(core, own, both, rows, out):
    left = own[:, 0, :].astype(F32)
    left = by_zh(jnp.concatenate([left[:, :TILE], left[:, TILE:]], axis=0))
    left = chunks(left, COLS)
    first = lax.broadcasted_iota(jnp.int32, left.shape, 0) % 8 < 4
    left = jnp.concatenate([jnp.where(first, left, 0.0), jnp.where(first, 0.0, left)], axis=1).astype(BF16)
    right = by_zh(both[:, 1, :].astype(F32))
    right = jnp.concatenate([chunks(right[:, :TILE], COLS), chunks(right[:, TILE:], COLS)], axis=1)
    right = jnp.dot(rows[...], right.astype(BF16), preferred_element_type=F32).astype(BF16)
    sums = lax.dot_general(left, right, (((1,), (1,)), ((), ())), preferred_element_type=F32)
    pack(sums, out)


def by_column(side):
    return jnp.concatenate(
        [side[c * PAIRS + g * 4 : c * PAIRS + (g + 1) * 4] for g in range(16) for c in range(2)], axis=0
    )


def incoming_kernel(core, both, rows, out):
    def operand(side, wide):
        return jnp.concatenate(
            [
                jnp.concatenate(
                    [side[g * 8 : (g + 1) * 8, k * COLS : k * COLS + wide] for g in range(16)], axis=1
                )
                for k in range(ROWS)
            ],
            axis=0,
        ).astype(BF16)

    left = by_column(both[:, 0, :].astype(F32))
    left = jnp.where(core[0] == 0, left, jnp.concatenate([left[:, ROWS:], left[:, :ROWS]], axis=1))
    left = [operand(left[:, i * TILE : (i + 1) * TILE], COLS // 2) for i in range(2)]
    left = [
        lax.dot_general(rows[...], left[i], (((1,), (1,)), ((), ())), preferred_element_type=F32)
        for i in range(2)
    ]
    zero = jnp.zeros_like(left[0])
    left = [jnp.concatenate([left[0], zero], axis=1), jnp.concatenate([zero, left[1]], axis=1)]
    left = [v[g * 4 : (g + 1) * 4] for g in range(4 * ROWS) for v in left]
    left = jnp.concatenate(left, axis=0).astype(BF16)
    right = by_column(both[:, 1, :].astype(F32))
    right = [operand(right[:, i * TILE : (i + 1) * TILE], COLS) for i in range(2)]
    sums = jnp.dot(left, jnp.concatenate(right, axis=0), preferred_element_type=F32)
    pack(sums, out)


def add_kernel(added, got, out):
    parts = []
    for i in range(4):
        total = 0.0
        for j in range(4):
            total += got[j * 4 + i if added == 0 else i * 4 + j].astype(F32)
        parts.append(unfold(total))
    total = jnp.concatenate(parts, axis=1)
    for i in range(2):
        rows = [total[zh * 8 + i * 4 : zh * 8 + i * 4 + 4] for zh in range(4)]
        out[:, i, :] = jnp.concatenate(rows, axis=0).astype(BF16)


def call(kernel, name, n_in, *shapes, scalars=0):
    out = [jax.ShapeDtypeStruct(s, BF16) for s in shapes]
    spaces = [pltpu.SMEM] * scalars + [pltpu.VMEM] * (n_in - scalars)
    return pl.pallas_call(
        kernel,
        in_specs=[pl.BlockSpec(memory_space=space) for space in spaces],
        out_shape=out if len(out) > 1 else out[0],
        name=name,
        compiler_params=pltpu.CompilerParams(vmem_limit_bytes=32 * 1024 * 1024),
    )


def call_first(*operands):
    return pl.pallas_call(
        first_kernel,
        in_specs=[pl.BlockSpec(memory_space=pltpu.HBM)] * len(operands),
        out_shape=[
            jax.ShapeDtypeStruct((PAIRS, 2, 2 * TILE), BF16),
            jax.ShapeDtypeStruct((4, WIDTH), F32),
        ],
        scratch_shapes=[
            pltpu.VMEM((TILE, WIDTH), BF16),
            pltpu.VMEM((ROWS, COLS), jnp.int32),
            pltpu.VMEM((WIDTH, 4 * WIDTH), BF16),
            pltpu.SemaphoreType.DMA((7,)),
        ],
        name="project_first",
        compiler_params=pltpu.CompilerParams(vmem_limit_bytes=60 * 1024 * 1024),
    )(*operands)


def per_device(
    pair_input,
    pair_mask,
    out_norm_gain,
    out_w_in,
    out_final_gain,
    out_w_out,
    in_norm_gain,
    in_w_in,
    in_final_gain,
    in_w_out,
):
    out_norm_gain, out_final_gain, in_norm_gain, in_final_gain = (
        g.reshape(1, WIDTH) for g in (out_norm_gain, out_final_gain, in_norm_gain, in_final_gain)
    )
    out_rows = one_hot(reorder((ROWS, 4, 2, 4), (3, 1, 2, 0)))
    in_rows = one_hot(reorder((4, 4, ROWS), (2, 1, 0)))
    out_rows, in_rows = (
        jnp.asarray(t) for t in (out_rows, in_rows)
    )
    core = lax.axis_index("core").reshape(1).astype(jnp.int32)

    def spread(sent, order):
        got = lax.all_to_all(sent, order, 0, 0, tiled=True)
        return got, lax.all_gather(got, "core", tiled=True)

    def collect(pieces, added):
        got = lax.all_to_all(pieces, PLANE, 0, 0, tiled=True)
        add = functools.partial(add_kernel, added)
        sums = call(add, "add_parts", 1, (16, 2, 4 * TILE))(got)
        return lax.all_to_all(sums, LINE, 0, 0, tiled=True)

    pair = pair_input.reshape(TILE, WIDTH)
    sent, gains = call_first(
        pair,
        pair_mask,
        out_norm_gain,
        out_final_gain,
        in_norm_gain,
        in_final_gain,
        out_w_in,
    )
    own, both = spread(sent, OUT_CHANNEL)
    pieces = call(outgoing_kernel, "outgoing", 4, (16, 72, 128), scalars=1)(core, own, both, out_rows)
    tri = collect(pieces, 0)

    middle, sent = call(middle_kernel, "middle", 7, (TILE, WIDTH), (PAIRS, 2, 2 * TILE))(
        pair, pair_mask, tri, gains, out_w_in, out_w_out, in_w_in
    )
    _, both = spread(sent, IN_CHANNEL)
    pieces = call(incoming_kernel, "incoming", 3, (16, 72, 128), scalars=1)(
        core, both, in_rows
    )
    tri = collect(pieces, 1)
    out = call(last_kernel, "last", 5, (TILE, WIDTH))(middle, tri, gains, in_w_in, in_w_out)
    return out.reshape(ROWS, COLS, WIDTH)


def solution(mesh):
    fine = Mesh(
        mesh.devices.reshape([SIZES[a] for a in ROW + COL]), ROW + COL
    )
    placed = (P(ROW, COL, None), P(ROW, COL), P(), P(), P(), P(), P(), P(), P(), P())
    return jax.shard_map(
        per_device, mesh=fine, in_specs=placed, out_specs=P(ROW, COL, None), check_vma=False
    )
```

```python
import functools

import jax
import jax.numpy as jnp
import ml_dtypes
import numpy as np
from jax import lax
from jax.experimental import pallas as pl
from jax.experimental.pallas import tpu as pltpu
from jax.sharding import Mesh
from jax.sharding import PartitionSpec as P

ROW = ("zl", "y", "core")
COL = ("x", "zh")
SIZES = {"zl": 4, "y": 4, "core": 2, "x": 4, "zh": 4}
OUT_CHANNEL = ("y", "zh", "zl")
IN_CHANNEL = ("x", "zh", "zl")
LINE = ("zh", "zl")
PLANE = ("x", "y")

ROWS, COLS, WIDTH = 12, 24, 128
TILE = ROWS * COLS
PAIRS = WIDTH // 2
N = 384
F32, BF16 = jnp.float32, jnp.bfloat16


def one_hot(places, width=None):
    places = np.asarray(places).reshape(-1)
    table = np.zeros((len(places), width or len(places)), np.float32)
    table[np.arange(len(places))[places >= 0], places[places >= 0]] = 1
    return table.astype(ml_dtypes.bfloat16)


def reorder(sizes, order):
    return np.arange(np.prod(sizes)).reshape(sizes).transpose(order)


def layer_norm(values, gain):
    center = values - jnp.mean(values, axis=-1, keepdims=True)
    spread = jnp.mean(center * center, axis=-1, keepdims=True)
    return center * lax.rsqrt(spread + 1e-05) * gain


def flat_mask(mask):
    return jnp.concatenate([mask[i : i + 1] for i in range(ROWS)], axis=1)


def project(normed, mask, w_in):
    proj = lax.dot_general(
        w_in[:, : 4 * WIDTH], normed, (((0,), (1,)), ((), ())), preferred_element_type=F32
    )
    left = proj[:WIDTH] * jax.nn.sigmoid(proj[2 * WIDTH : 3 * WIDTH]) * mask
    right = proj[WIDTH : 2 * WIDTH] * jax.nn.sigmoid(proj[3 * WIDTH : 4 * WIDTH]) * mask
    return [jnp.concatenate([v[:PAIRS], v[PAIRS:]], axis=1).astype(BF16) for v in (left, right)]


def update(pair, tri, norm_gain, w_in, final_gain, w_out):
    final = layer_norm(tri.T, final_gain).astype(BF16)
    normed = layer_norm(pair, norm_gain).astype(BF16)
    gate = jax.nn.sigmoid(jnp.dot(normed, w_in[:, 4 * WIDTH :], preferred_element_type=F32))
    return (pair + jnp.dot(final, w_out, preferred_element_type=F32) * gate).astype(BF16)


def sums_of(tri):
    pair = [tri[:, i, :].astype(F32) for i in range(2)]
    return jnp.concatenate([v[:, i * TILE : (i + 1) * TILE] for v in pair for i in range(4)], axis=0)


def first_kernel(pair_ref, mask_ref, g0, g1, g2, g3, w_in, sent, gains, pair, mask, weights, sems):
    copies = [
        pltpu.make_async_copy(pair_ref, pair, sems.at[0]),
        pltpu.make_async_copy(mask_ref, mask, sems.at[1]),
        pltpu.make_async_copy(w_in.at[:, pl.ds(0, 4 * WIDTH)], weights, sems.at[2]),
    ]
    for i, gain in enumerate((g0, g1, g2, g3)):
        copies.append(pltpu.make_async_copy(gain, gains.at[pl.ds(i, 1)], sems.at[3 + i]))
    for copy in copies:
        copy.start()
    for copy in copies:
        copy.wait()
    normed = layer_norm(pair[...].astype(F32), gains[0:1]).astype(BF16)
    sent[:, 0, :], sent[:, 1, :] = project(normed, flat_mask(mask[...].astype(F32)), weights[...])


def middle_kernel(pair_ref, mask, tri, gains, w_in, w_out, next_w_in, middle, sent):
    pair = pair_ref[...].astype(F32)
    new = update(pair, sums_of(tri), gains[0:1], w_in, gains[1:2], w_out[...])
    middle[...] = new
    normed = layer_norm(new.astype(F32), gains[2:3]).astype(BF16)
    sent[:, 0, :], sent[:, 1, :] = project(normed, flat_mask(mask[...].astype(F32)), next_w_in)


def last_kernel(pair_ref, tri, gains, w_in, w_out, out):
    pair = pair_ref[...].astype(F32)
    out[...] = update(pair, sums_of(tri), gains[2:3], w_in, gains[3:4], w_out[...])


def chunks(side, wide):
    return jnp.concatenate(
        [
            jnp.concatenate([side[x * 32 : (x + 1) * 32, i * wide : (i + 1) * wide] for x in range(4)], axis=1)
            for i in range(ROWS)
        ],
        axis=0,
    )


def fold(strip):
    n = strip.shape[0] // 4
    rest = jnp.concatenate([strip[g * n : (g + 1) * n, 256:] for g in range(4)], axis=1)
    return jnp.concatenate([strip[:, :128], strip[:, 128:256], rest], axis=0)


def unfold(folded):
    n = folded.shape[0] // 9
    rest = jnp.concatenate([folded[8 * n :, g * 32 : (g + 1) * 32] for g in range(4)], axis=0)
    return jnp.concatenate([folded[: 4 * n], folded[4 * n : 8 * n], rest], axis=1)


def pack(sums, out):
    for x in range(4):
        strips = []
        for zh in range(4):
            at = (x * 4 + zh) * COLS
            strips.append(
                jnp.concatenate([sums[i * 32 : (i + 1) * 32, at : at + COLS] for i in range(ROWS)], axis=1)
            )
        for y in range(4):
            piece = jnp.concatenate([s[y * 8 : (y + 1) * 8] for s in strips], axis=0)
            out[x * 4 + y] = fold(piece).astype(BF16)


def by_zh(side):
    starts = [c * PAIRS + y * 16 + zh * 4 for zh in range(4) for y in range(4) for c in range(2)]
    return jnp.concatenate([side[i : i + 4] for i in starts], axis=0)


def outgoing_kernel(core, own, both, rows, out):
    left = own[:, 0, :].astype(F32)
    left = by_zh(jnp.concatenate([left[:, :TILE], left[:, TILE:]], axis=0))
    left = chunks(left, COLS)
    first = lax.broadcasted_iota(jnp.int32, left.shape, 0) % 8 < 4
    left = jnp.concatenate([jnp.where(first, left, 0.0), jnp.where(first, 0.0, left)], axis=1).astype(BF16)
    right = by_zh(both[:, 1, :].astype(F32))
    right = jnp.concatenate([chunks(right[:, :TILE], COLS), chunks(right[:, TILE:], COLS)], axis=1)
    blocks = []
    for y in range(4):
        block = [right[i * 32 + y * 8 : i * 32 + (y + 1) * 8] for i in range(ROWS)]
        block = jnp.concatenate(block, axis=0).astype(BF16)
        blocks.append(jnp.dot(rows[...], block, preferred_element_type=F32))
    right = [b[zl * 24 : (zl + 1) * 24] for zl in range(4) for b in blocks]
    right = jnp.concatenate(right, axis=0).astype(BF16)
    sums = lax.dot_general(left, right, (((1,), (1,)), ((), ())), preferred_element_type=F32)
    pack(sums, out)


def by_column(side):
    return jnp.concatenate(
        [side[c * PAIRS + g * 4 : c * PAIRS + (g + 1) * 4] for g in range(16) for c in range(2)], axis=0
    )


def incoming_kernel(core, both, rows, out):
    def operand(side, wide):
        return jnp.concatenate(
            [
                jnp.concatenate(
                    [side[g * 8 : (g + 1) * 8, k * COLS : k * COLS + wide] for g in range(16)], axis=1
                )
                for k in range(ROWS)
            ],
            axis=0,
        ).astype(BF16)

    left = by_column(both[:, 0, :].astype(F32))
    left = jnp.where(core[0] == 0, left, jnp.concatenate([left[:, ROWS:], left[:, :ROWS]], axis=1))
    left = [operand(left[:, i * TILE : (i + 1) * TILE], COLS // 2) for i in range(2)]
    left = [
        lax.dot_general(rows[...], left[i], (((1,), (1,)), ((), ())), preferred_element_type=F32)
        for i in range(2)
    ]
    zero = jnp.zeros_like(left[0])
    left = [jnp.concatenate([left[0], zero], axis=1), jnp.concatenate([zero, left[1]], axis=1)]
    left = [v[g * 4 : (g + 1) * 4] for g in range(4 * ROWS) for v in left]
    left = jnp.concatenate(left, axis=0).astype(BF16)
    right = by_column(both[:, 1, :].astype(F32))
    right = [operand(right[:, i * TILE : (i + 1) * TILE], COLS) for i in range(2)]
    sums = jnp.dot(left, jnp.concatenate(right, axis=0), preferred_element_type=F32)
    pack(sums, out)


def add_kernel(added, got, out):
    parts = []
    for i in range(4):
        total = 0.0
        for j in range(4):
            total += got[j * 4 + i if added == 0 else i * 4 + j].astype(F32)
        parts.append(unfold(total))
    total = jnp.concatenate(parts, axis=1)
    for i in range(2):
        rows = [total[zh * 8 + i * 4 : zh * 8 + i * 4 + 4] for zh in range(4)]
        out[:, i, :] = jnp.concatenate(rows, axis=0).astype(BF16)


def call(kernel, name, n_in, *shapes, scalars=0):
    out = [jax.ShapeDtypeStruct(s, BF16) for s in shapes]
    spaces = [pltpu.SMEM] * scalars + [pltpu.VMEM] * (n_in - scalars)
    return pl.pallas_call(
        kernel,
        in_specs=[pl.BlockSpec(memory_space=space) for space in spaces],
        out_shape=out if len(out) > 1 else out[0],
        name=name,
        compiler_params=pltpu.CompilerParams(vmem_limit_bytes=32 * 1024 * 1024),
    )


def call_first(*operands):
    return pl.pallas_call(
        first_kernel,
        in_specs=[pl.BlockSpec(memory_space=pltpu.HBM)] * len(operands),
        out_shape=[
            jax.ShapeDtypeStruct((PAIRS, 2, 2 * TILE), BF16),
            jax.ShapeDtypeStruct((4, WIDTH), F32),
        ],
        scratch_shapes=[
            pltpu.VMEM((TILE, WIDTH), BF16),
            pltpu.VMEM((ROWS, COLS), jnp.int32),
            pltpu.VMEM((WIDTH, 4 * WIDTH), BF16),
            pltpu.SemaphoreType.DMA((7,)),
        ],
        name="project_first",
        compiler_params=pltpu.CompilerParams(vmem_limit_bytes=60 * 1024 * 1024),
    )(*operands)


def per_device(
    pair_input,
    pair_mask,
    out_norm_gain,
    out_w_in,
    out_final_gain,
    out_w_out,
    in_norm_gain,
    in_w_in,
    in_final_gain,
    in_w_out,
):
    out_norm_gain, out_final_gain, in_norm_gain, in_final_gain = (
        g.reshape(1, WIDTH) for g in (out_norm_gain, out_final_gain, in_norm_gain, in_final_gain)
    )
    out_rows = one_hot(reorder((ROWS, 2, 4), (2, 1, 0)))
    in_rows = one_hot(reorder((4, 4, ROWS), (2, 1, 0)))
    out_rows, in_rows = (
        jnp.asarray(t) for t in (out_rows, in_rows)
    )
    core = lax.axis_index("core").reshape(1).astype(jnp.int32)

    def spread(sent, order):
        got = lax.all_to_all(sent, order, 0, 0, tiled=True)
        return got, lax.all_gather(got, "core", tiled=True)

    def collect(pieces, added):
        got = lax.all_to_all(pieces, PLANE, 0, 0, tiled=True)
        add = functools.partial(add_kernel, added)
        sums = call(add, "add_parts", 1, (16, 2, 4 * TILE))(got)
        return lax.all_to_all(sums, LINE, 0, 0, tiled=True)

    pair = pair_input.reshape(TILE, WIDTH)
    sent, gains = call_first(
        pair,
        pair_mask,
        out_norm_gain,
        out_final_gain,
        in_norm_gain,
        in_final_gain,
        out_w_in,
    )
    own, both = spread(sent, OUT_CHANNEL)
    pieces = call(outgoing_kernel, "outgoing", 4, (16, 72, 128), scalars=1)(core, own, both, out_rows)
    tri = collect(pieces, 0)

    middle, sent = call(middle_kernel, "middle", 7, (TILE, WIDTH), (PAIRS, 2, 2 * TILE))(
        pair, pair_mask, tri, gains, out_w_in, out_w_out, in_w_in
    )
    _, both = spread(sent, IN_CHANNEL)
    pieces = call(incoming_kernel, "incoming", 3, (16, 72, 128), scalars=1)(
        core, both, in_rows
    )
    tri = collect(pieces, 1)
    out = call(last_kernel, "last", 5, (TILE, WIDTH))(middle, tri, gains, in_w_in, in_w_out)
    return out.reshape(ROWS, COLS, WIDTH)


def solution(mesh):
    fine = Mesh(
        mesh.devices.reshape([SIZES[a] for a in ROW + COL]), ROW + COL
    )
    placed = (P(ROW, COL, None), P(ROW, COL), P(), P(), P(), P(), P(), P(), P(), P())
    return jax.shard_map(
        per_device, mesh=fine, in_specs=placed, out_specs=P(ROW, COL, None), check_vma=False
    )
```
